32 devices in a mesh: slab: 16 (over z, x, core), plane: 2 (over y).
Axes of the slice: x: 2, y: 2, z: 4, core: 2. Of those that a mesh axis runs over, the one named last changes fastest.
Arguments:
- probe_pos: bfloat16 [3, 4096], P(None, ('slab', 'plane')), may hold values from 0 to 2
- atom_pos: bfloat16 [3, 4096], P(None, ('slab', 'plane')), may hold values from 0 to 2
- atom_feat: bfloat16 [128, 4096], P(None, ('slab', 'plane')), may hold values from -6 to 6
- neighbours: int32 [32, 4096], P(None, ('slab', 'plane')), may hold values from 0 to 4095, as said below
- valid: int32 [32, 4096], P(None, ('slab', 'plane')), may hold values 0 or 1
- w_radial1: float32 [64, 8], replicated, may hold values from -2 to 2
- w_radial2: bfloat16 [640, 64], replicated, may hold values from -0.75 to 0.75
- readout: float32 [5, 128], replicated, may hold values from -0.5 to 0.5
- cotangent: float32 [4096], P(('slab', 'plane')), may hold values from -6 to 6
Outputs:
- density: float32 [4096], P(('slab', 'plane'))
- grad_feat: float32 [128, 4096], P(None, ('slab', 'plane'))
- grad_radial1: float32 [64, 8], replicated
- grad_radial2: float32 [640, 64], replicated
- grad_readout: float32 [5, 128], replicated
The draws below stay inside these ranges and needn't reach their ends.
Inputs may be any that keep to these rules, and one draw needn't show every extreme that they name: `neighbours`: the atom of every slot of probe p lies in the slab of p (atoms a with a // 256 = p // 256) or in one of the two slabs beside it on the periodic cycle of slabs.
All inputs are finite; a program needn't handle non-finite values. No bound on the sum of `valid` on one device may be relied on, other than what follows from the above.
Results may differ from the reference program's by a relative error of at most 0.0049.
Values may be sent and summed in bfloat16 or wider, within the bound.
A program may use at most 128 MiB of HBM per device.

```python
import math
import jax
import jax.numpy as jnp
from jax import lax

C = 128
DEG = 5
NB = 8
RH = 64
NBR = 32
PROBE_DEV = 128
ATOM_SLAB = 256
ATOMS = 4096
PROBE_SLAB = 256
PROBES = 4096
N_SLAB = 16


def draw_neighbours(key, part):
    key_offset, key_local = jax.random.split(key)
    offset = jax.random.randint(key_offset, (NBR, PROBES), -1, 2)
    local_row = jax.random.randint(key_local, (NBR, PROBES), 0, ATOM_SLAB)
    slab_of = jnp.arange(PROBES, dtype=jnp.int32) // PROBE_SLAB
    return ((slab_of[None, :] + offset) % N_SLAB * ATOM_SLAB + local_row).astype(jnp.int32)


def plant(drawn, rng, least, top_value):
    index_at = [jax.random.randint(jax.random.fold_in(rng, axis), (), 0, length) for axis, length in enumerate(drawn.shape)]
    longest = drawn.shape.index(max(drawn.shape))
    neighbour = index_at[:longest] + [(index_at[longest] + 1) % drawn.shape[longest]] + index_at[longest + 1:]
    return drawn.at[tuple(index_at)].set(least).at[tuple(neighbour)].set(top_value)


def block_scale(own_key, dims, cuts, low, top_value):
    def one(position, blocks):
        steps = jax.random.uniform(jax.random.fold_in(jax.random.fold_in(own_key, 6), position), (blocks,), jnp.float32, low / len(cuts), top_value / len(cuts))
        return jnp.repeat(jnp.exp(steps), dims[position] // blocks).reshape((-1,) + (1,) * (len(dims) - position - 1))

    level = one(*cuts[0])
    for cut in cuts[1:]:
        level = level * one(*cut)
    return level


def bell_draw(own_key, dims, spread, reach, shards=(), kind=jnp.bfloat16):
    drawn = jax.random.normal(own_key, dims, jnp.float32) * spread
    if len(shards) > 0:
        drawn = block_scale(own_key, dims, shards, -0.22, 0.18) * drawn
    return jnp.clip(drawn, min=-reach, max=reach).astype(kind)


def setup_inputs(seed: int = 0) -> dict:
    streams_of = jax.random.split(jax.random.key(seed), 10)
    probe_pos = jnp.clip(2.0 * jax.random.uniform(streams_of[0], (3, PROBES), jnp.float32) ** block_scale(streams_of[0], (3, PROBES), ((1, 32),), -0.2, 0.2), 0.0, 2.0).astype(jnp.bfloat16)
    atom_pos = jnp.clip(2.0 * jax.random.uniform(streams_of[1], (3, ATOMS), jnp.float32) ** block_scale(streams_of[1], (3, ATOMS), ((1, 32),), -0.2, 0.2), 0.0, 2.0).astype(jnp.bfloat16)
    atom_feat = bell_draw(streams_of[2], (C, ATOMS), 1.0, 6.0, ((1, 32),))
    neighbours = draw_neighbours(jax.random.fold_in(streams_of[9], 71), 0)
    valid = plant((jax.random.randint(streams_of[4], (NBR, PROBES), 0, 4) < 3).astype(jnp.int32), jax.random.fold_in(streams_of[4], 1), 0, 1)
    w_radial1 = bell_draw(streams_of[5], (RH, NB), NB ** -0.5, 2.0, (), jnp.float32)
    w_radial2 = bell_draw(streams_of[6], (DEG * C, RH), RH ** -0.5, 0.75)
    readout = bell_draw(streams_of[7], (DEG, C), C ** -0.5, 0.5, (), jnp.float32)
    cotangent = bell_draw(streams_of[8], (PROBES,), 1.0, 6.0, ((0, 32),), jnp.float32)
    return {"probe_pos": probe_pos, "atom_pos": atom_pos, "atom_feat": atom_feat, "neighbours": neighbours, "valid": valid, "w_radial1": w_radial1, "w_radial2": w_radial2, "readout": readout, "cotangent": cotangent}


slab_width = 2.0
soften = 0.25

def harmonics(along_x, along_y, along_z):
    sq_x = along_x * along_x
    sq_y = along_y * along_y
    sq_z = along_z * along_z
    root3 = math.sqrt(3.0)
    root15 = math.sqrt(15.0)
    root5 = math.sqrt(5.0)
    coef_a1 = math.sqrt(35.0 / 8.0)
    coef_a2 = math.sqrt(105.0)
    coef_a3 = math.sqrt(21.0 / 8.0)
    coef_a4 = math.sqrt(7.0) / 2.0
    coef_b1 = 3.0 * math.sqrt(35.0) / 2.0
    coef_b2 = 3.0 * math.sqrt(70.0) / 4.0
    coef_b3 = 3.0 * math.sqrt(5.0) / 2.0
    coef_b4 = 3.0 * math.sqrt(10.0) / 4.0
    rows_out = [jnp.ones_like(along_x), root3 * along_y, root3 * along_z, root3 * along_x, root15 * along_x * along_y, root15 * along_y * along_z, root5 / 2.0 * (3.0 * sq_z - 1.0), root15 * along_x * along_z, root15 / 2.0 * (sq_x - sq_y), coef_a1 * along_y * (3.0 * sq_x - sq_y), coef_a2 * along_x * along_y * along_z, coef_a3 * along_y * (5.0 * sq_z - 1.0), coef_a4 * along_z * (5.0 * sq_z - 3.0), coef_a3 * along_x * (5.0 * sq_z - 1.0), coef_a2 / 2.0 * along_z * (sq_x - sq_y), coef_a1 * along_x * (sq_x - 3.0 * sq_y), coef_b1 * along_x * along_y * (sq_x - sq_y), coef_b2 * along_y * along_z * (3.0 * sq_x - sq_y), coef_b3 * along_x * along_y * (7.0 * sq_z - 1.0), coef_b4 * along_y * along_z * (7.0 * sq_z - 3.0), 0.375 * (35.0 * sq_z * sq_z - 30.0 * sq_z + 3.0), coef_b4 * along_x * along_z * (7.0 * sq_z - 3.0), coef_b3 / 2.0 * (sq_x - sq_y) * (7.0 * sq_z - 1.0), coef_b2 * along_x * along_z * (sq_x - 3.0 * sq_y), coef_b1 / 4.0 * (sq_x * (sq_x - 3.0 * sq_y) - sq_y * (3.0 * sq_x - sq_y))]
    return jnp.stack(rows_out)

def probe_block(features, atom_xyz, probe_xyz, offset, weight_mask, cot_block, w_radial1, w_radial2, readout):
    slots, block_len = weight_mask.shape
    edge_count = slots * block_len
    channels = features.shape[0]
    degrees = readout.shape[0]
    probe_tile = jnp.broadcast_to(probe_xyz[:, None, :], (3, slots, block_len)).reshape(3, edge_count)
    delta_x = atom_xyz[0] - probe_tile[0]
    delta_y = atom_xyz[1] - probe_tile[1]
    delta_z = atom_xyz[2] + slab_width * offset.reshape(edge_count) - probe_tile[2]
    radius = jnp.sqrt(delta_x * delta_x + delta_y * delta_y + delta_z * delta_z + soften)
    sphere = harmonics(delta_x / radius, delta_y / radius, delta_z / radius)
    centres = 0.75 * jnp.arange(w_radial1.shape[1], dtype=jnp.float32)
    radial_basis = jnp.exp(-2.0 * (radius[None, :] - centres[:, None]) ** 2)
    preact = jnp.dot(w_radial1, radial_basis, precision=lax.Precision.HIGHEST)
    hidden = jax.nn.silu(preact).astype(jnp.bfloat16)
    radial = jnp.dot(w_radial2, hidden, preferred_element_type=jnp.float32).reshape(degrees, channels, edge_count)
    weight = weight_mask.reshape(edge_count) * (1.0 / math.sqrt(slots))
    feat_float = features.astype(jnp.float32)
    messages = (radial * feat_float[None] * weight[None, None, :]).reshape(degrees, channels, slots, block_len)
    sphere_rows = sphere.reshape(degrees * degrees, slots, block_len)
    density = jnp.zeros((block_len,), jnp.float32)
    grad_msg = []
    grad_read = []
    for degree in range(degrees):
        part_y = sphere_rows[degree * degree:(degree + 1) * (degree + 1)]
        moment = jnp.einsum('kjp,cjp->kcp', part_y, messages[degree], precision=lax.Precision.HIGHEST)
        if degree == 0:
            density = density + lax.optimization_barrier(jnp.sum(readout[0][:, None] * moment[0], axis=0))
            grad_mom = jnp.broadcast_to(cot_block[None, None, :] * readout[0][None, :, None], moment.shape)
            grad_read.append(lax.optimization_barrier(jnp.sum(cot_block[None, :] * moment[0], axis=1)))
        else:
            squares = lax.optimization_barrier(jnp.sum(moment * moment, axis=0))
            density = density + lax.optimization_barrier(jnp.sum(readout[degree][:, None] * squares, axis=0))
            grad_mom = 2.0 * cot_block[None, None, :] * readout[degree][None, :, None] * moment
            grad_read.append(lax.optimization_barrier(jnp.sum(cot_block[None, :] * squares, axis=1)))
        grad_msg.append(jnp.einsum('kjp,kcp->cjp', part_y, grad_mom, precision=lax.Precision.HIGHEST))
    grad_messages = jnp.stack(grad_msg).reshape(degrees, channels, edge_count)
    grad_features = lax.optimization_barrier(jnp.sum(grad_messages * radial, axis=0)) * weight[None, :]
    grad_radial = (grad_messages * feat_float[None] * weight[None, None, :]).reshape(degrees * channels, edge_count).astype(jnp.bfloat16)
    grad_w2 = lax.dot_general(grad_radial, hidden, (((1,), (1,)), ((), ())), preferred_element_type=jnp.float32)
    grad_hidden = lax.dot_general(w_radial2, grad_radial, (((0,), (0,)), ((), ())), preferred_element_type=jnp.float32)
    logistic = jax.nn.sigmoid(preact)
    grad_pre = grad_hidden * logistic * (1.0 + preact * (1.0 - logistic))
    grad_w1 = lax.dot_general(grad_pre, radial_basis, (((1,), (1,)), ((), ())), precision=lax.Precision.HIGHEST)
    return (density, grad_features, grad_w1, grad_w2, jnp.stack(grad_read))

def reference(probe_pos, atom_pos, atom_feat, neighbours, valid, w_radial1, w_radial2, readout, cotangent):
    block_len = 128 if PROBE_DEV % 128 == 0 else PROBE_DEV
    count = PROBES // block_len
    probe_float = probe_pos.astype(jnp.float32)

    def advance(totals, number):
        grad_atoms, total_w1, total_w2, total_read = totals
        first_probe = number * block_len
        atom_rows = lax.dynamic_slice_in_dim(neighbours, first_probe, block_len, 1)
        mask_float = lax.dynamic_slice_in_dim(valid, first_probe, block_len, 1).astype(jnp.float32)
        probe_xyz = lax.dynamic_slice_in_dim(probe_float, first_probe, block_len, 1)
        cot_block = lax.dynamic_slice_in_dim(cotangent, first_probe, block_len, 0)
        flat_rows = atom_rows.reshape(-1)
        features = jnp.take(atom_feat, flat_rows, axis=1)
        atom_xyz = jnp.take(atom_pos, flat_rows, axis=1).astype(jnp.float32)
        probe_slab = (first_probe + jnp.arange(block_len, dtype=jnp.int32)) // PROBE_SLAB
        atom_slab = atom_rows // ATOM_SLAB
        offset = ((atom_slab - probe_slab[None, :] + 1) % N_SLAB - 1).astype(jnp.float32)
        density, grad_features, grad_w1, grad_w2, grad_read = probe_block(features, atom_xyz, probe_xyz, offset, mask_float, cot_block, w_radial1, w_radial2, readout)
        grad_atoms = grad_atoms.at[:, flat_rows].add(grad_features)
        return ((grad_atoms, total_w1 + grad_w1, total_w2 + grad_w2, total_read + grad_read), density)
    start_totals = (jnp.zeros((C, ATOMS), jnp.float32), jnp.zeros((RH, NB), jnp.float32), jnp.zeros((DEG * C, RH), jnp.float32), jnp.zeros((DEG, C), jnp.float32))
    totals, densities = lax.scan(advance, start_totals, jnp.arange(count, dtype=jnp.int32))
    scale = 1.0 / math.sqrt(PROBES)
    return (densities.reshape(-1), totals[0], totals[1] * scale, totals[2] * scale, totals[3] * scale)
```

```python
import functools
import math

import jax
import jax.numpy as jnp
from jax import lax
from jax.experimental import pallas as pl
from jax.experimental.pallas import tpu as pltpu
from jax.sharding import PartitionSpec as P

slab_width = 2.0
soften = 0.25
f32 = jnp.float32
bf16 = jnp.bfloat16
MESH = pl.DeviceIdType.MESH
HIGH = lax.Precision.HIGHEST
VMEM = pl.BlockSpec(memory_space=pltpu.VMEM)
NT = (((1,), (1,)), ((), ()))
TN = (((0,), (0,)), ((), ()))


def harmonics(x, y, z):
    xx, yy, zz = x * x, y * y, z * z
    r3, r5, r15 = math.sqrt(3.0), math.sqrt(5.0), math.sqrt(15.0)
    a1, a2 = math.sqrt(35.0 / 8.0), math.sqrt(105.0)
    a3, a4 = math.sqrt(21.0 / 8.0), math.sqrt(7.0) / 2.0
    b1, b2 = 3.0 * math.sqrt(35.0) / 2.0, 3.0 * math.sqrt(70.0) / 4.0
    b3, b4 = 3.0 * math.sqrt(5.0) / 2.0, 3.0 * math.sqrt(10.0) / 4.0
    return [
        jnp.ones_like(x),
        r3 * y,
        r3 * z,
        r3 * x,
        r15 * x * y,
        r15 * y * z,
        r5 / 2.0 * (3.0 * zz - 1.0),
        r15 * x * z,
        r15 / 2.0 * (xx - yy),
        a1 * y * (3.0 * xx - yy),
        a2 * x * y * z,
        a3 * y * (5.0 * zz - 1.0),
        a4 * z * (5.0 * zz - 3.0),
        a3 * x * (5.0 * zz - 1.0),
        a2 / 2.0 * z * (xx - yy),
        a1 * x * (xx - 3.0 * yy),
        b1 * x * y * (xx - yy),
        b2 * y * z * (3.0 * xx - yy),
        b3 * x * y * (7.0 * zz - 1.0),
        b4 * y * z * (7.0 * zz - 3.0),
        0.375 * (35.0 * zz * zz - 30.0 * zz + 3.0),
        b4 * x * z * (7.0 * zz - 3.0),
        b3 / 2.0 * (xx - yy) * (7.0 * zz - 1.0),
        b2 * x * z * (xx - 3.0 * yy),
        b1 / 4.0 * (xx * (xx - 3.0 * yy) - yy * (3.0 * xx - yy)),
    ]


def halo_peers(n_slab, n_plane):
    slab, plane = lax.axis_index("slab"), lax.axis_index("plane")
    peers = []
    for d in (-1, 0, 1):
        for q in range(n_plane):
            if d == 0 and q == 0:
                continue
            to_slab = lax.rem(slab + d + n_slab, n_slab)
            to_plane = lax.rem(plane + q, n_plane)
            peers.append((d, q, to_slab, to_plane))
    return slab, plane, peers


def halo_kernel(n_slab, n_plane, own_ref, out_ref, land, send_sem, recv_sem):
    slab, plane, peers = halo_peers(n_slab, n_plane)
    barrier = pltpu.get_barrier_semaphore()
    for _, _, to_slab, to_plane in peers:
        pl.semaphore_signal(barrier, inc=1, device_id=(to_slab, to_plane), device_id_type=MESH)
    pl.semaphore_wait(barrier, len(peers))
    copies = []
    for number, (d, _, to_slab, to_plane) in enumerate(peers):
        copy = pltpu.make_async_remote_copy(
            src_ref=own_ref,
            dst_ref=land.at[(1 - d) * n_plane + plane],
            send_sem=send_sem.at[number],
            recv_sem=recv_sem.at[number],
            device_id=(to_slab, to_plane),
            device_id_type=MESH,
        )
        copy.start()
        copies.append(copy)
    land[n_plane + plane] = own_ref[...]
    for copy in copies:
        copy.wait()
    out_ref[...] = land[...]


def edge_kernel(
    n_slab,
    n_plane,
    win_ref,
    nbr_ref,
    valid_ref,
    probe_ref,
    cot_ref,
    w1_ref,
    w2_ref,
    read_ref,
    readt_ref,
    dens_ref,
    gwin_ref,
    pack_ref,
    win,
    rows_s,
    wgt,
    xyz,
    onehot,
    feat,
    gfeat,
    sph,
    sphb,
    rad_s,
    basis,
    pre,
    hid,
    radial,
    gradial,
    squares,
    gwin_acc,
    gw2_acc,
    gw1_acc,
):
    slots, probes = nbr_ref.shape
    blocks, _, atoms = win_ref.shape
    width = blocks * atoms
    atom_slab = n_plane * atoms
    channels = feat.shape[0]
    degrees = read_ref.shape[0]
    per = 4
    chunk = per * probes
    chunks = slots // per
    total = n_slab * atom_slab
    for b in range(blocks):
        win[:, b * atoms : (b + 1) * atoms] = win_ref[b]
    local = nbr_ref[...] - (lax.axis_index("slab") - 1) * atom_slab
    local = jnp.where(local < 0, local + total, local)
    local = jnp.where(local >= total, local - total, local)
    rows_s[...] = local
    wgt[...] = valid_ref[...].astype(f32) * (1.0 / math.sqrt(slots))
    offset = jnp.where(local < atom_slab, -1.0, jnp.where(local < 2 * atom_slab, 0.0, 1.0))
    atom_iota = lax.broadcasted_iota(jnp.int32, (width, probes), 0)

    def gather(i, _):
        for s in range(per):
            row = rows_s[pl.ds(i * per + s, 1), :]
            at = pl.multiple_of(i * chunk + s * probes, probes)
            onehot[:, pl.ds(at, probes)] = (atom_iota == row).astype(f32).astype(bf16)
        at = pl.multiple_of(i * chunk, chunk)
        got = jnp.dot(win[...], onehot[:, pl.ds(at, chunk)], preferred_element_type=f32)
        for s in range(per):
            j = i * per + s
            part = got[:, s * probes : (s + 1) * probes]
            at = pl.multiple_of(i * chunk + s * probes, probes)
            feat[:, pl.ds(at, probes)] = part[:channels] * wgt[pl.ds(j, 1), :]
            for k in range(3):
                xyz[k, pl.ds(j, 1), :] = part[channels + k : channels + k + 1]
        return 0

    lax.fori_loop(0, chunks, gather, 0)

    probe = probe_ref[...].astype(f32)
    dx = xyz[0] - probe[0:1]
    dy = xyz[1] - probe[1:2]
    dz = xyz[2] + slab_width * offset - probe[2:3]
    radius = jnp.sqrt(dx * dx + dy * dy + dz * dz + soften)
    rad_s[...] = radius
    for k, row in enumerate(harmonics(dx / radius, dy / radius, dz / radius)):
        sph[k] = row
    rows_k = degrees * degrees
    sph[rows_k] = wgt[...]

    n_basis = w1_ref.shape[1]
    centres = 0.75 * lax.broadcasted_iota(jnp.int32, (n_basis, probes), 0).astype(f32)

    def spread(j, _):
        for k in range(rows_k + 1):
            sphb[j, k] = jnp.broadcast_to(sph[k, pl.ds(j, 1), :], (8, probes))
        shift = rad_s[pl.ds(j, 1), :] - centres
        basis[:, pl.ds(pl.multiple_of(j * probes, probes), probes)] = jnp.exp(
            -2.0 * (shift * shift)
        )
        return 0

    lax.fori_loop(0, slots, spread, 0)

    def network(i, _):
        at = pl.ds(pl.multiple_of(i * chunk, chunk), chunk)
        value = jnp.dot(w1_ref[...], basis[:, at], precision=HIGH, preferred_element_type=f32)
        pre[:, at] = value
        hidden = (value * jax.nn.sigmoid(value)).astype(bf16)
        hid[:, at] = hidden
        radial[:, at] = jnp.dot(w2_ref[...], hidden, preferred_element_type=f32)
        return 0

    lax.fori_loop(0, chunks, network, 0)

    cot = jnp.broadcast_to(cot_ref[...], (8, probes))

    def channel_tile(t, dens):
        c0 = pl.multiple_of(t * 8, 8)

        def forward(j, acc):
            at = pl.ds(pl.multiple_of(j * probes, probes), probes)
            scaled = feat[pl.ds(c0, 8), at]
            acc = list(acc)
            for l in range(degrees):
                message = radial[pl.ds(l * channels + c0, 8), at] * scaled
                for k in range(l * l, (l + 1) * (l + 1)):
                    acc[k] = acc[k] + (message if k == 0 else sphb[j, k] * message)
            return tuple(acc)

        zero = jnp.zeros((8, probes), f32)
        moment = lax.fori_loop(0, slots, forward, (zero,) * rows_k, unroll=4)
        grad = []
        for l in range(degrees):
            column = jnp.broadcast_to(readt_ref[pl.ds(c0, 8), l : l + 1], (8, probes))
            if l == 0:
                squared = moment[0]
                grad.append(cot * column)
            else:
                squared = moment[l * l] * moment[l * l]
                for k in range(l * l + 1, (l + 1) * (l + 1)):
                    squared = squared + moment[k] * moment[k]
                factor = 2.0 * cot * column
                for k in range(l * l, (l + 1) * (l + 1)):
                    grad.append(factor * moment[k])
            squares[l, pl.ds(c0, 8), :] = squared
            dens = dens + column * squared

        def backward(j, carry):
            at = pl.ds(pl.multiple_of(j * probes, probes), probes)
            scaled = feat[pl.ds(c0, 8), at]
            total_feat = None
            for l in range(degrees):
                message = None
                for k in range(l * l, (l + 1) * (l + 1)):
                    term = grad[k] if k == 0 else sphb[j, k] * grad[k]
                    message = term if message is None else message + term
                here = pl.ds(l * channels + c0, 8)
                term = message * radial[here, at]
                total_feat = term if total_feat is None else total_feat + term
                gradial[here, at] = message * scaled
            gfeat[pl.ds(c0, 8), at] = total_feat * sphb[j, rows_k]
            return carry

        lax.fori_loop(0, slots, backward, 0, unroll=4)
        return dens

    dens = lax.fori_loop(0, channels // 8, channel_tile, jnp.zeros((8, probes), f32))
    dens_ref[...] = jnp.sum(dens, axis=0, keepdims=True)

    gwin_acc[...] = jnp.zeros_like(gwin_acc)
    gw2_acc[...] = jnp.zeros_like(gw2_acc)
    gw1_acc[...] = jnp.zeros_like(gw1_acc)

    def weights(i, _):
        at = pl.ds(pl.multiple_of(i * chunk, chunk), chunk)
        grads = gradial[:, at].astype(bf16)
        gw2_acc[...] += lax.dot_general(grads, hid[:, at], NT, preferred_element_type=f32)
        ghid = lax.dot_general(w2_ref[...], grads, TN, preferred_element_type=f32)
        value = pre[:, at]
        logistic = jax.nn.sigmoid(value)
        gpre = ghid * logistic * (1.0 + value * (1.0 - logistic))
        gw1_acc[...] += lax.dot_general(
            basis[:, at], gpre, NT, precision=HIGH, preferred_element_type=f32
        )
        gwin_acc[...] += lax.dot_general(
            gfeat[:, at].astype(bf16), onehot[:, at], NT, preferred_element_type=f32
        )
        return 0

    lax.fori_loop(0, chunks, weights, 0)

    for b in range(blocks):
        gwin_ref[b] = gwin_acc[:, b * atoms : (b + 1) * atoms].astype(bf16)
    half, hidden_units = gw2_acc.shape[0] // 2, gw2_acc.shape[1]
    lines = jnp.concatenate([gw2_acc[:half], gw2_acc[half:]], axis=1)
    small = []
    for l in range(degrees):
        small.append(
            lax.dot_general(cot, squares[l], NT, precision=HIGH, preferred_element_type=f32)[:1]
        )
    small.append(jnp.zeros((8 - degrees, channels), f32))
    first = jnp.concatenate(small, axis=0)
    second = jnp.concatenate(
        [gw1_acc[...], jnp.zeros((n_basis, channels - hidden_units), f32)], axis=1
    )
    pack_ref[0:half] = lines.astype(bf16)
    pack_ref[half : half + 16] = jnp.concatenate([first, second], axis=0).astype(bf16)
    rest = pack_ref.shape[0] - half - 16
    pack_ref[half + 16 :] = jnp.zeros((rest, channels), bf16)


def reduce_kernel(
    n_slab,
    n_plane,
    low,
    gwin_ref,
    pack_ref,
    gfeat_ref,
    out_ref,
    land,
    part_b,
    part_c,
    land_a,
    land_b,
    land_c,
    halo_send,
    halo_recv,
    a_send,
    a_recv,
    b_send,
    b_recv,
    c_send,
    c_recv,
):
    slab, plane, peers = halo_peers(n_slab, n_plane)
    group, high = low * n_plane, n_slab // low
    size = pack_ref.shape[0] // group
    slab_low, slab_high = lax.rem(slab, low), slab // low
    me = slab_low * n_plane + plane
    near = []
    for t in range(1, group):
        to = lax.rem(me + t, group)
        near.append((to, (slab - slab_low + to // n_plane, lax.rem(to, n_plane))))
    far = []
    for t in range(1, high):
        to = lax.rem(slab_high + t, high)
        far.append((to * low + slab_low, plane))
    barrier = pltpu.get_barrier_semaphore()
    everyone = [(p[2], p[3]) for p in peers] + [n[1] for n in near] + far
    for device in everyone:
        pl.semaphore_signal(barrier, inc=1, device_id=device, device_id_type=MESH)
    pl.semaphore_wait(barrier, len(everyone))

    def send(source, target, send_sem, recv_sem, device):
        copy = pltpu.make_async_remote_copy(
            src_ref=source,
            dst_ref=target,
            send_sem=send_sem,
            recv_sem=recv_sem,
            device_id=device,
            device_id_type=MESH,
        )
        copy.start()
        return copy

    first = []
    for t, (to, device) in enumerate(near):
        rows = pl.ds(pl.multiple_of(to * size, 16), size)
        first.append(send(pack_ref.at[rows], land_a.at[t], a_send.at[t], a_recv.at[t], device))
    halo = []
    for t, (d, _, to_slab, to_plane) in enumerate(peers):
        halo.append(
            send(
                gwin_ref.at[(d + 1) * n_plane + to_plane],
                land.at[(d + 1) * n_plane + plane],
                halo_send.at[t],
                halo_recv.at[t],
                (to_slab, to_plane),
            )
        )
    land[n_plane + plane] = gwin_ref[n_plane + plane]
    total = pack_ref[pl.ds(pl.multiple_of(me * size, 16), size)].astype(f32)
    for t, copy in enumerate(first):
        copy.wait_recv()
        total = total + land_a[t].astype(f32)
    part_b[...] = total
    land_b[slab_high] = total
    second = []
    for t, device in enumerate(far):
        second.append(
            send(part_b, land_b.at[slab_high], b_send.at[t], b_recv.at[t], device)
        )
    for copy in second:
        copy.wait_recv()
    total = land_b[0]
    for t in range(1, high):
        total = total + land_b[t]
    part_c[...] = total.astype(bf16)
    land_c[me] = total.astype(bf16)
    third = []
    for t, (_, device) in enumerate(near):
        third.append(send(part_c, land_c.at[me], c_send.at[t], c_recv.at[t], device))
    for copy in halo:
        copy.wait_recv()
    gfeat = land[0].astype(f32)
    for b in range(1, land.shape[0]):
        gfeat = gfeat + land[b].astype(f32)
    gfeat_ref[...] = gfeat
    for copy in third:
        copy.wait_recv()
    for b in range(group):
        out_ref[b * size : (b + 1) * size] = land_c[b].astype(f32)
    for copy in first + halo + second + third:
        copy.wait_send()


def shards(
    n_slab,
    n_plane,
    probe_pos,
    atom_pos,
    atom_feat,
    neighbours,
    valid,
    w_radial1,
    w_radial2,
    readout,
    cotangent,
):
    channels, atoms = atom_feat.shape
    slots, probes = neighbours.shape
    units, n_basis = w_radial1.shape
    degrees = readout.shape[0]
    out_rows = w_radial2.shape[0]
    half = out_rows // 2
    edges = slots * probes
    blocks = 3 * n_plane
    lines = -(-(channels + atom_pos.shape[0]) // 16) * 16
    peers = blocks - 1
    own = jnp.concatenate(
        [atom_feat, atom_pos, jnp.zeros((lines - channels - atom_pos.shape[0], atoms), bf16)], axis=0
    )
    window = pl.pallas_call(
        functools.partial(halo_kernel, n_slab, n_plane),
        out_shape=jax.ShapeDtypeStruct((blocks, lines, atoms), bf16),
        in_specs=[VMEM],
        out_specs=VMEM,
        scratch_shapes=[
            pltpu.VMEM((blocks, lines, atoms), bf16),
            pltpu.SemaphoreType.DMA((peers,)),
            pltpu.SemaphoreType.DMA((peers,)),
        ],
        compiler_params=pltpu.CompilerParams(collective_id=0, has_side_effects=True),
        name="halo",
    )(own)
    low = 4 if n_slab % 4 == 0 else 1
    group, high = low * n_plane, n_slab // low
    size = -(-(half + 16) // (16 * group)) * 16
    width = blocks * atoms
    kinds = degrees * degrees + 1
    density, gwin, pack = pl.pallas_call(
        functools.partial(edge_kernel, n_slab, n_plane),
        out_shape=(
            jax.ShapeDtypeStruct((1, probes), f32),
            jax.ShapeDtypeStruct((blocks, channels, atoms), bf16),
            jax.ShapeDtypeStruct((size * group, channels), bf16),
        ),
        in_specs=[VMEM] * 9,
        out_specs=(VMEM,) * 3,
        scratch_shapes=[
            pltpu.VMEM((lines, width), bf16),
            pltpu.VMEM((slots, probes), jnp.int32),
            pltpu.VMEM((slots, probes), f32),
            pltpu.VMEM((3, slots, probes), f32),
            pltpu.VMEM((width, edges), bf16),
            pltpu.VMEM((channels, edges), f32),
            pltpu.VMEM((channels, edges), f32),
            pltpu.VMEM((kinds, slots, probes), f32),
            pltpu.VMEM((slots, kinds, 8, probes), f32),
            pltpu.VMEM((slots, probes), f32),
            pltpu.VMEM((n_basis, edges), f32),
            pltpu.VMEM((units, edges), f32),
            pltpu.VMEM((units, edges), bf16),
            pltpu.VMEM((out_rows, edges), f32),
            pltpu.VMEM((out_rows, edges), f32),
            pltpu.VMEM((degrees, channels, probes), f32),
            pltpu.VMEM((channels, width), f32),
            pltpu.VMEM((out_rows, units), f32),
            pltpu.VMEM((n_basis, units), f32),
        ],
        compiler_params=pltpu.CompilerParams(vmem_limit_bytes=52 * 1024 * 1024),
        name="edges",
    )(
        window,
        neighbours,
        valid,
        probe_pos,
        cotangent.reshape(1, probes),
        w_radial1,
        w_radial2,
        readout,
        readout.T,
    )
    grad_feat, summed = pl.pallas_call(
        functools.partial(reduce_kernel, n_slab, n_plane, low),
        out_shape=(
            jax.ShapeDtypeStruct((channels, atoms), f32),
            jax.ShapeDtypeStruct((size * group, channels), f32),
        ),
        in_specs=[VMEM] * 2,
        out_specs=(VMEM,) * 2,
        scratch_shapes=[
            pltpu.VMEM((blocks, channels, atoms), bf16),
            pltpu.VMEM((size, channels), f32),
            pltpu.VMEM((size, channels), bf16),
            pltpu.VMEM((group - 1, size, channels), bf16),
            pltpu.VMEM((high, size, channels), f32),
            pltpu.VMEM((group, size, channels), bf16),
            pltpu.SemaphoreType.DMA((peers,)),
            pltpu.SemaphoreType.DMA((peers,)),
            pltpu.SemaphoreType.DMA((group - 1,)),
            pltpu.SemaphoreType.DMA((group - 1,)),
            pltpu.SemaphoreType.DMA((high,)),
            pltpu.SemaphoreType.DMA((high,)),
            pltpu.SemaphoreType.DMA((group - 1,)),
            pltpu.SemaphoreType.DMA((group - 1,)),
        ],
        compiler_params=pltpu.CompilerParams(collective_id=1, has_side_effects=True),
        name="reduce",
    )(gwin, pack)
    scale = 1.0 / math.sqrt(probes * n_slab * n_plane)
    grad_w2 = jnp.concatenate([summed[:half, :units], summed[:half, units:]], axis=0) * scale
    grad_read = summed[half : half + degrees] * scale
    grad_w1 = summed[half + 8 : half + 8 + n_basis, :units].T * scale
    return density.reshape(-1), grad_feat, grad_w1, grad_w2, grad_read


def solution(mesh):
    both = P(None, ("slab", "plane"))
    in_specs = (both,) * 5 + (P(), P(), P(), P(("slab", "plane")))
    out_specs = (P(("slab", "plane")), both, P(), P(), P())
    body = functools.partial(shards, mesh.shape["slab"], mesh.shape["plane"])
    return jax.shard_map(
        body, mesh=mesh, in_specs=in_specs, out_specs=out_specs, check_vma=False
    )
```

```python
import functools
import math

import jax
import jax.numpy as jnp
from jax import lax
from jax.experimental import pallas as pl
from jax.experimental.pallas import tpu as pltpu
from jax.sharding import PartitionSpec as P

slab_width = 2.0
soften = 0.25
f32 = jnp.float32
bf16 = jnp.bfloat16
MESH = pl.DeviceIdType.MESH
HIGH = lax.Precision.HIGHEST
VMEM = pl.BlockSpec(memory_space=pltpu.VMEM)
NT = (((1,), (1,)), ((), ()))


def harmonics(x, y, z):
    xx, yy, zz = x * x, y * y, z * z
    r3, r5, r15 = math.sqrt(3.0), math.sqrt(5.0), math.sqrt(15.0)
    a1, a2 = math.sqrt(35.0 / 8.0), math.sqrt(105.0)
    a3, a4 = math.sqrt(21.0 / 8.0), math.sqrt(7.0) / 2.0
    b1, b2 = 3.0 * math.sqrt(35.0) / 2.0, 3.0 * math.sqrt(70.0) / 4.0
    b3, b4 = 3.0 * math.sqrt(5.0) / 2.0, 3.0 * math.sqrt(10.0) / 4.0
    return [
        jnp.ones_like(x),
        r3 * y,
        r3 * z,
        r3 * x,
        r15 * x * y,
        r15 * y * z,
        r5 / 2.0 * (3.0 * zz - 1.0),
        r15 * x * z,
        r15 / 2.0 * (xx - yy),
        a1 * y * (3.0 * xx - yy),
        a2 * x * y * z,
        a3 * y * (5.0 * zz - 1.0),
        a4 * z * (5.0 * zz - 3.0),
        a3 * x * (5.0 * zz - 1.0),
        a2 / 2.0 * z * (xx - yy),
        a1 * x * (xx - 3.0 * yy),
        b1 * x * y * (xx - yy),
        b2 * y * z * (3.0 * xx - yy),
        b3 * x * y * (7.0 * zz - 1.0),
        b4 * y * z * (7.0 * zz - 3.0),
        0.375 * (35.0 * zz * zz - 30.0 * zz + 3.0),
        b4 * x * z * (7.0 * zz - 3.0),
        b3 / 2.0 * (xx - yy) * (7.0 * zz - 1.0),
        b2 * x * z * (xx - 3.0 * yy),
        b1 / 4.0 * (xx * (xx - 3.0 * yy) - yy * (3.0 * xx - yy)),
    ]


def halo_peers(n_slab, n_plane):
    slab, plane = lax.axis_index("slab"), lax.axis_index("plane")
    peers = []
    for d in (-1, 0, 1):
        for q in range(n_plane):
            if d == 0 and q == 0:
                continue
            to_slab = lax.rem(slab + d + n_slab, n_slab)
            to_plane = lax.rem(plane + q, n_plane)
            peers.append((d, q, to_slab, to_plane))
    return slab, plane, peers


def halo_kernel(n_slab, n_plane, feat_ref, pos_ref, out_ref, own, land, send_sem, recv_sem):
    slab, plane, peers = halo_peers(n_slab, n_plane)
    barrier = pltpu.get_barrier_semaphore()
    for _, _, to_slab, to_plane in peers:
        pl.semaphore_signal(barrier, inc=1, device_id=(to_slab, to_plane), device_id_type=MESH)
    channels = feat_ref.shape[0]
    rest = own.shape[0] - channels - pos_ref.shape[0]
    own[0:channels] = feat_ref[...]
    own[channels:] = jnp.concatenate(
        [pos_ref[...].astype(f32), jnp.zeros((rest, own.shape[1]), f32)], axis=0
    ).astype(bf16)
    pl.semaphore_wait(barrier, len(peers))
    copies = []
    for number, (d, _, to_slab, to_plane) in enumerate(peers):
        copy = pltpu.make_async_remote_copy(
            src_ref=own,
            dst_ref=land.at[(1 - d) * n_plane + plane],
            send_sem=send_sem.at[number],
            recv_sem=recv_sem.at[number],
            device_id=(to_slab, to_plane),
            device_id_type=MESH,
        )
        copy.start()
        copies.append(copy)
    land[n_plane + plane] = own[...]
    for copy in copies:
        copy.wait()
    out_ref[...] = land[...]


def edge_kernel(
    n_slab,
    n_plane,
    win_ref,
    nbr_ref,
    valid_ref,
    probe_ref,
    cot_ref,
    w1t_ref,
    w2t_ref,
    read_ref,
    dens_ref,
    gwin_ref,
    pack_ref,
    win,
    rows_s,
    wgt,
    xyz,
    onehot,
    feat,
    gfeat,
    sph,
    sphb,
    rad_s,
    basis,
    pre,
    hid,
    radial,
    gradial,
    squares,
    gwin_acc,
    gw2_acc,
    gw1_acc,
    readt,
    w1,
    w2,
):
    slots, probes = nbr_ref.shape
    blocks, _, atoms = win_ref.shape
    width = blocks * atoms
    atom_slab = n_plane * atoms
    channels = feat.shape[0]
    degrees = read_ref.shape[0]
    per = 4
    chunk = per * probes
    chunks = slots // per
    total = n_slab * atom_slab
    for b in range(blocks):
        win[:, b * atoms : (b + 1) * atoms] = win_ref[b]
    local = nbr_ref[...] - (lax.axis_index("slab") - 1) * atom_slab
    local = jnp.where(local < 0, local + total, local)
    local = jnp.where(local >= total, local - total, local)
    rows_s[...] = local
    wgt[...] = valid_ref[...].astype(f32) * (1.0 / math.sqrt(slots))
    offset = jnp.where(local < atom_slab, -1.0, jnp.where(local < 2 * atom_slab, 0.0, 1.0))
    atom_iota = lax.broadcasted_iota(jnp.int32, (width, probes), 0)

    readt[...] = jnp.concatenate(
        [read_ref[...], jnp.zeros((8 - degrees, channels), f32)], axis=0
    ).T
    n_basis, units = w1t_ref.shape
    w1[...] = jnp.concatenate(
        [w1t_ref[...], jnp.zeros((n_basis, channels - units), f32)], axis=1
    ).T[:units]
    w2[...] = w2t_ref[...].astype(f32).T.astype(bf16)

    for i in range(chunks):
        for s in range(per):
            row = rows_s[i * per + s : i * per + s + 1, :]
            at = i * chunk + s * probes
            onehot[:, at : at + probes] = (atom_iota == row).astype(f32).astype(bf16)
        here = slice(i * chunk, (i + 1) * chunk)
        got = jnp.dot(win[...], onehot[:, here], preferred_element_type=f32)
        for s in range(per):
            j = i * per + s
            part = got[:, s * probes : (s + 1) * probes]
            at = i * chunk + s * probes
            feat[:, at : at + probes] = part[:channels] * wgt[j : j + 1, :]
            for k in range(3):
                xyz[k, j : j + 1, :] = part[channels + k : channels + k + 1]

    probe = probe_ref[...].astype(f32)
    dx = xyz[0] - probe[0:1]
    dy = xyz[1] - probe[1:2]
    dz = xyz[2] + slab_width * offset - probe[2:3]
    radius = jnp.sqrt(dx * dx + dy * dy + dz * dz + soften)
    rad_s[...] = radius
    for k, row in enumerate(harmonics(dx / radius, dy / radius, dz / radius)):
        sph[k] = row
    rows_k = degrees * degrees
    sph[rows_k] = wgt[...]
    centres = 0.75 * lax.broadcasted_iota(jnp.int32, (n_basis, probes), 0).astype(f32)

    for j in range(slots):
        shift = rad_s[j : j + 1, :] - centres
        basis[:, j * probes : (j + 1) * probes] = jnp.exp(-2.0 * (shift * shift))

    for i in range(chunks):
        at = slice(i * chunk, (i + 1) * chunk)
        for j in range(i * per, (i + 1) * per):
            for k in range(rows_k + 1):
                sphb[j, k] = jnp.broadcast_to(sph[k, j : j + 1, :], (8, probes))
        value = jnp.dot(w1[...], basis[:, at], precision=HIGH, preferred_element_type=f32)
        pre[:, at] = value
        hidden = (value * jax.nn.sigmoid(value)).astype(bf16)
        hid[:, at] = hidden
        radial[:, at] = jnp.dot(w2[...], hidden, preferred_element_type=f32)

    cot = jnp.broadcast_to(cot_ref[...], (8, probes))

    def channel_tile(t, dens):
        c0 = pl.multiple_of(t * 8, 8)

        def forward(j, acc):
            at = pl.ds(pl.multiple_of(j * probes, probes), probes)
            scaled = feat[pl.ds(c0, 8), at]
            acc = list(acc)
            for l in range(degrees):
                message = radial[pl.ds(l * channels + c0, 8), at] * scaled
                for k in range(l * l, (l + 1) * (l + 1)):
                    acc[k] = acc[k] + (message if k == 0 else sphb[j, k] * message)
            return tuple(acc)

        zero = jnp.zeros((8, probes), f32)
        moment = lax.fori_loop(0, slots, forward, (zero,) * rows_k, unroll=4)
        grad = []
        for l in range(degrees):
            column = jnp.broadcast_to(readt[pl.ds(c0, 8), l : l + 1], (8, probes))
            if l == 0:
                squared = moment[0]
                grad.append(cot * column)
            else:
                squared = moment[l * l] * moment[l * l]
                for k in range(l * l + 1, (l + 1) * (l + 1)):
                    squared = squared + moment[k] * moment[k]
                factor = 2.0 * cot * column
                for k in range(l * l, (l + 1) * (l + 1)):
                    grad.append(factor * moment[k])
            squares[l, pl.ds(c0, 8), :] = squared
            dens = dens + column * squared

        def backward(j, carry):
            at = pl.ds(pl.multiple_of(j * probes, probes), probes)
            scaled = feat[pl.ds(c0, 8), at]
            total_feat = None
            for l in range(degrees):
                message = None
                for k in range(l * l, (l + 1) * (l + 1)):
                    term = grad[k] if k == 0 else sphb[j, k] * grad[k]
                    message = term if message is None else message + term
                here = pl.ds(l * channels + c0, 8)
                term = message * radial[here, at]
                total_feat = term if total_feat is None else total_feat + term
                gradial[here, at] = message * scaled
            gfeat[pl.ds(c0, 8), at] = total_feat * sphb[j, rows_k]
            return carry

        lax.fori_loop(0, slots, backward, 0, unroll=4)
        return dens

    dens = lax.fori_loop(0, channels // 8, channel_tile, jnp.zeros((8, probes), f32))
    dens_ref[...] = jnp.sum(dens, axis=0, keepdims=True)

    gwin_acc[...] = jnp.zeros_like(gwin_acc)
    gw2_acc[...] = jnp.zeros_like(gw2_acc)
    gw1_acc[...] = jnp.zeros_like(gw1_acc)

    for i in range(chunks):
        at = slice(i * chunk, (i + 1) * chunk)
        grads = gradial[:, at].astype(bf16)
        gw2_acc[...] += lax.dot_general(hid[:, at], grads, NT, preferred_element_type=f32)
        ghid = jnp.dot(w2t_ref[...], grads, preferred_element_type=f32)
        value = pre[:, at]
        logistic = jax.nn.sigmoid(value)
        gpre = ghid * logistic * (1.0 + value * (1.0 - logistic))
        gw1_acc[...] += lax.dot_general(
            basis[:, at], gpre, NT, precision=HIGH, preferred_element_type=f32
        )
        gwin_acc[...] += lax.dot_general(
            gfeat[:, at].astype(bf16), onehot[:, at], NT, preferred_element_type=f32
        )

    for b in range(blocks):
        gwin_ref[b] = gwin_acc[:, b * atoms : (b + 1) * atoms].astype(bf16)
    for l in range(degrees):
        pack_ref[l * units : (l + 1) * units] = gw2_acc[
            :, l * channels : (l + 1) * channels
        ].astype(bf16)
    half = degrees * units
    small = []
    for l in range(degrees):
        small.append(
            lax.dot_general(cot, squares[l], NT, precision=HIGH, preferred_element_type=f32)[:1]
        )
    small.append(jnp.zeros((8 - degrees, channels), f32))
    first = jnp.concatenate(small, axis=0)
    second = jnp.concatenate(
        [gw1_acc[...], jnp.zeros((n_basis, channels - units), f32)], axis=1
    )
    pack_ref[half : half + 16] = jnp.concatenate([first, second], axis=0).astype(bf16)
    rest = pack_ref.shape[0] - half - 16
    pack_ref[half + 16 :] = jnp.zeros((rest, channels), bf16)


def reduce_kernel(
    n_slab,
    n_plane,
    low,
    scale,
    gwin_ref,
    pack_ref,
    gfeat_ref,
    gw1_ref,
    gw2_ref,
    gread_ref,
    full,
    land,
    part_b,
    part_c,
    land_a,
    land_b,
    land_c,
    halo_send,
    halo_recv,
    a_send,
    a_recv,
    b_send,
    b_recv,
    c_send,
    c_recv,
):
    slab, plane, peers = halo_peers(n_slab, n_plane)
    group, high = low * n_plane, n_slab // low
    size = pack_ref.shape[0] // group
    slab_low, slab_high = lax.rem(slab, low), slab // low
    me = slab_low * n_plane + plane
    near = []
    for t in range(1, group):
        to = lax.rem(me + t, group)
        near.append((to, (slab - slab_low + to // n_plane, lax.rem(to, n_plane))))
    far = []
    for t in range(1, high):
        to = lax.rem(slab_high + t, high)
        far.append((to * low + slab_low, plane))
    barrier = pltpu.get_barrier_semaphore()
    everyone = [(p[2], p[3]) for p in peers] + [n[1] for n in near] + far
    for device in everyone:
        pl.semaphore_signal(barrier, inc=1, device_id=device, device_id_type=MESH)
    pl.semaphore_wait(barrier, len(everyone))

    def send(source, target, send_sem, recv_sem, device):
        copy = pltpu.make_async_remote_copy(
            src_ref=source,
            dst_ref=target,
            send_sem=send_sem,
            recv_sem=recv_sem,
            device_id=device,
            device_id_type=MESH,
        )
        copy.start()
        return copy

    first = []
    for t, (to, device) in enumerate(near):
        rows = pl.ds(pl.multiple_of(to * size, 16), size)
        first.append(send(pack_ref.at[rows], land_a.at[t], a_send.at[t], a_recv.at[t], device))
    halo = []
    for t, (d, _, to_slab, to_plane) in enumerate(peers):
        halo.append(
            send(
                gwin_ref.at[(d + 1) * n_plane + to_plane],
                land.at[(d + 1) * n_plane + plane],
                halo_send.at[t],
                halo_recv.at[t],
                (to_slab, to_plane),
            )
        )
    land[n_plane + plane] = gwin_ref[n_plane + plane]
    total = pack_ref[pl.ds(pl.multiple_of(me * size, 16), size)].astype(f32)
    for t, copy in enumerate(first):
        copy.wait_recv()
        total = total + land_a[t].astype(f32)
    part_b[...] = total
    land_b[slab_high] = total
    second = []
    for t, device in enumerate(far):
        second.append(
            send(part_b, land_b.at[slab_high], b_send.at[t], b_recv.at[t], device)
        )
    for copy in second:
        copy.wait_recv()
    total = land_b[0]
    for t in range(1, high):
        total = total + land_b[t]
    part_c[...] = total.astype(bf16)
    land_c[me] = total.astype(bf16)
    third = []
    for t, (_, device) in enumerate(near):
        third.append(send(part_c, land_c.at[me], c_send.at[t], c_recv.at[t], device))
    for copy in halo:
        copy.wait_recv()
    gfeat = land[0].astype(f32)
    for b in range(1, land.shape[0]):
        gfeat = gfeat + land[b].astype(f32)
    gfeat_ref[...] = gfeat
    for copy in third:
        copy.wait_recv()
    for b in range(group):
        full[b * size : (b + 1) * size] = land_c[b].astype(f32) * scale
    units, channels = gw2_ref.shape[0], gwin_ref.shape[1]
    degrees = gw2_ref.shape[1] // channels
    for l in range(degrees):
        gw2_ref[:, l * channels : (l + 1) * channels] = full[l * units : (l + 1) * units]
    half = degrees * units
    gread_ref[...] = full[half : half + gread_ref.shape[0]]
    gw1_ref[...] = full[half + 8 : half + 8 + gw1_ref.shape[0], 0:units]
    for copy in first + halo + second + third:
        copy.wait_send()


def shards(
    n_slab,
    n_plane,
    probe_pos,
    atom_pos,
    atom_feat,
    neighbours,
    valid,
    w_radial1,
    w_radial2,
    readout,
    cotangent,
):
    channels, atoms = atom_feat.shape
    slots, probes = neighbours.shape
    units, n_basis = w_radial1.shape
    degrees = readout.shape[0]
    out_rows = w_radial2.shape[0]
    half = degrees * units
    edges = slots * probes
    blocks = 3 * n_plane
    lines = -(-(channels + atom_pos.shape[0]) // 16) * 16
    peers = blocks - 1
    window = pl.pallas_call(
        functools.partial(halo_kernel, n_slab, n_plane),
        out_shape=jax.ShapeDtypeStruct((blocks, lines, atoms), bf16),
        in_specs=[VMEM] * 2,
        out_specs=VMEM,
        scratch_shapes=[
            pltpu.VMEM((lines, atoms), bf16),
            pltpu.VMEM((blocks, lines, atoms), bf16),
            pltpu.SemaphoreType.DMA((peers,)),
            pltpu.SemaphoreType.DMA((peers,)),
        ],
        compiler_params=pltpu.CompilerParams(collective_id=0, has_side_effects=True),
        name="halo",
    )(atom_feat, atom_pos)
    low = 4 if n_slab % 4 == 0 else 1
    group, high = low * n_plane, n_slab // low
    size = -(-(half + 16) // (16 * group)) * 16
    width = blocks * atoms
    kinds = degrees * degrees + 1
    density, gwin, pack = pl.pallas_call(
        functools.partial(edge_kernel, n_slab, n_plane),
        out_shape=(
            jax.ShapeDtypeStruct((1, probes), f32),
            jax.ShapeDtypeStruct((blocks, channels, atoms), bf16),
            jax.ShapeDtypeStruct((size * group, channels), bf16),
        ),
        in_specs=[VMEM] * 8,
        out_specs=(VMEM,) * 3,
        scratch_shapes=[
            pltpu.VMEM((lines, width), bf16),
            pltpu.VMEM((slots, probes), jnp.int32),
            pltpu.VMEM((slots, probes), f32),
            pltpu.VMEM((3, slots, probes), f32),
            pltpu.VMEM((width, edges), bf16),
            pltpu.VMEM((channels, edges), f32),
            pltpu.VMEM((channels, edges), f32),
            pltpu.VMEM((kinds, slots, probes), f32),
            pltpu.VMEM((slots, kinds, 8, probes), f32),
            pltpu.VMEM((slots, probes), f32),
            pltpu.VMEM((n_basis, edges), f32),
            pltpu.VMEM((units, edges), f32),
            pltpu.VMEM((units, edges), bf16),
            pltpu.VMEM((out_rows, edges), f32),
            pltpu.VMEM((out_rows, edges), f32),
            pltpu.VMEM((degrees, channels, probes), f32),
            pltpu.VMEM((channels, width), f32),
            pltpu.VMEM((units, out_rows), f32),
            pltpu.VMEM((n_basis, units), f32),
            pltpu.VMEM((channels, 8), f32),
            pltpu.VMEM((units, n_basis), f32),
            pltpu.VMEM((out_rows, units), bf16),
        ],
        compiler_params=pltpu.CompilerParams(vmem_limit_bytes=44 * 1024 * 1024),
        name="edges",
    )(
        window,
        neighbours,
        valid,
        probe_pos,
        cotangent.reshape(1, probes),
        w_radial1.T,
        w_radial2.T,
        readout,
    )
    scale = 1.0 / math.sqrt(probes * n_slab * n_plane)
    grad_feat, grad_w1, grad_w2, grad_read = pl.pallas_call(
        functools.partial(reduce_kernel, n_slab, n_plane, low, scale),
        out_shape=(
            jax.ShapeDtypeStruct((channels, atoms), f32),
            jax.ShapeDtypeStruct((n_basis, units), f32),
            jax.ShapeDtypeStruct((units, out_rows), f32),
            jax.ShapeDtypeStruct((degrees, channels), f32),
        ),
        in_specs=[VMEM] * 2,
        out_specs=(VMEM,) * 4,
        scratch_shapes=[
            pltpu.VMEM((size * group, channels), f32),
            pltpu.VMEM((blocks, channels, atoms), bf16),
            pltpu.VMEM((size, channels), f32),
            pltpu.VMEM((size, channels), bf16),
            pltpu.VMEM((group - 1, size, channels), bf16),
            pltpu.VMEM((high, size, channels), f32),
            pltpu.VMEM((group, size, channels), bf16),
            pltpu.SemaphoreType.DMA((peers,)),
            pltpu.SemaphoreType.DMA((peers,)),
            pltpu.SemaphoreType.DMA((group - 1,)),
            pltpu.SemaphoreType.DMA((group - 1,)),
            pltpu.SemaphoreType.DMA((high,)),
            pltpu.SemaphoreType.DMA((high,)),
            pltpu.SemaphoreType.DMA((group - 1,)),
            pltpu.SemaphoreType.DMA((group - 1,)),
        ],
        compiler_params=pltpu.CompilerParams(collective_id=1, has_side_effects=True),
        name="reduce",
    )(gwin, pack)
    return density.reshape(-1), grad_feat, grad_w1.T, grad_w2.T, grad_read


def solution(mesh):
    both = P(None, ("slab", "plane"))
    in_specs = (both,) * 5 + (P(), P(), P(), P(("slab", "plane")))
    out_specs = (P(("slab", "plane")), both, P(), P(), P())
    body = functools.partial(shards, mesh.shape["slab"], mesh.shape["plane"])
    return jax.shard_map(
        body, mesh=mesh, in_specs=in_specs, out_specs=out_specs, check_vma=False
    )
```

```python
import functools
import math

import jax
import jax.numpy as jnp
from jax import lax
from jax.experimental import pallas as pl
from jax.experimental.pallas import tpu as pltpu
from jax.sharding import PartitionSpec as P

slab_width = 2.0
soften = 0.25
f32 = jnp.float32
bf16 = jnp.bfloat16
MESH = pl.DeviceIdType.MESH
HIGH = lax.Precision.HIGHEST
VMEM = pl.BlockSpec(memory_space=pltpu.VMEM)
ANY = pl.BlockSpec(memory_space=pl.ANY)
NT = (((1,), (1,)), ((), ()))


def harmonics(x, y, z):
    xx, yy, zz = x * x, y * y, z * z
    r3, r5, r15 = math.sqrt(3.0), math.sqrt(5.0), math.sqrt(15.0)
    a1, a2 = math.sqrt(35.0 / 8.0), math.sqrt(105.0)
    a3, a4 = math.sqrt(21.0 / 8.0), math.sqrt(7.0) / 2.0
    b1, b2 = 3.0 * math.sqrt(35.0) / 2.0, 3.0 * math.sqrt(70.0) / 4.0
    b3, b4 = 3.0 * math.sqrt(5.0) / 2.0, 3.0 * math.sqrt(10.0) / 4.0
    return [
        jnp.ones_like(x),
        r3 * y,
        r3 * z,
        r3 * x,
        r15 * x * y,
        r15 * y * z,
        r5 / 2.0 * (3.0 * zz - 1.0),
        r15 * x * z,
        r15 / 2.0 * (xx - yy),
        a1 * y * (3.0 * xx - yy),
        a2 * x * y * z,
        a3 * y * (5.0 * zz - 1.0),
        a4 * z * (5.0 * zz - 3.0),
        a3 * x * (5.0 * zz - 1.0),
        a2 / 2.0 * z * (xx - yy),
        a1 * x * (xx - 3.0 * yy),
        b1 * x * y * (xx - yy),
        b2 * y * z * (3.0 * xx - yy),
        b3 * x * y * (7.0 * zz - 1.0),
        b4 * y * z * (7.0 * zz - 3.0),
        0.375 * (35.0 * zz * zz - 30.0 * zz + 3.0),
        b4 * x * z * (7.0 * zz - 3.0),
        b3 / 2.0 * (xx - yy) * (7.0 * zz - 1.0),
        b2 * x * z * (xx - 3.0 * yy),
        b1 / 4.0 * (xx * (xx - 3.0 * yy) - yy * (3.0 * xx - yy)),
    ]


def halo_peers(n_slab, n_plane):
    slab, plane = lax.axis_index("slab"), lax.axis_index("plane")
    peers = []
    for d in (-1, 0, 1):
        for q in range(n_plane):
            if d == 0 and q == 0:
                continue
            to_slab = lax.rem(slab + d + n_slab, n_slab)
            to_plane = lax.rem(plane + q, n_plane)
            peers.append((d, q, to_slab, to_plane))
    return slab, plane, peers


def halo_kernel(n_slab, n_plane, feat_ref, pos_ref, out_ref, own, land, send_sem, recv_sem):
    slab, plane, peers = halo_peers(n_slab, n_plane)
    barrier = pltpu.get_barrier_semaphore()
    for _, _, to_slab, to_plane in peers:
        pl.semaphore_signal(barrier, inc=1, device_id=(to_slab, to_plane), device_id_type=MESH)
    channels = feat_ref.shape[0]
    rest = own.shape[0] - channels - pos_ref.shape[0]
    own[0:channels] = feat_ref[...]
    own[channels:] = jnp.concatenate(
        [pos_ref[...].astype(f32), jnp.zeros((rest, own.shape[1]), f32)], axis=0
    ).astype(bf16)
    pl.semaphore_wait(barrier, len(peers))
    copies = []
    for number, (d, _, to_slab, to_plane) in enumerate(peers):
        copy = pltpu.make_async_remote_copy(
            src_ref=own,
            dst_ref=land.at[(1 - d) * n_plane + plane],
            send_sem=send_sem.at[number],
            recv_sem=recv_sem.at[number],
            device_id=(to_slab, to_plane),
            device_id_type=MESH,
        )
        copy.start()
        copies.append(copy)
    land[n_plane + plane] = own[...]
    for copy in copies:
        copy.wait()
    out_ref[...] = land[...]


def edge_kernel(
    n_slab,
    n_plane,
    win_ref,
    nbr_ref,
    valid_ref,
    probe_ref,
    cot_ref,
    w1t_ref,
    w2t_ref,
    read_ref,
    dens_ref,
    gwin_ref,
    pack_ref,
    win,
    rows_s,
    wgt,
    xyz,
    onehot,
    feat,
    gfeat,
    sph,
    sphb,
    rad_s,
    basis,
    pre,
    hid,
    radial,
    gradial,
    squares,
    gwin_acc,
    gw2_acc,
    gw1_acc,
    readt,
    w1,
    w2,
):
    slots, probes = nbr_ref.shape
    blocks, _, atoms = win_ref.shape
    width = blocks * atoms
    atom_slab = n_plane * atoms
    channels = feat.shape[0]
    degrees = read_ref.shape[0]
    per = 4
    chunk = per * probes
    chunks = slots // per
    total = n_slab * atom_slab
    for b in range(blocks):
        win[:, b * atoms : (b + 1) * atoms] = win_ref[b]
    local = nbr_ref[...] - (lax.axis_index("slab") - 1) * atom_slab
    local = jnp.where(local < 0, local + total, local)
    local = jnp.where(local >= total, local - total, local)
    rows_s[...] = local
    wgt[...] = valid_ref[...].astype(f32) * (1.0 / math.sqrt(slots))
    offset = jnp.where(local < atom_slab, -1.0, jnp.where(local < 2 * atom_slab, 0.0, 1.0))
    atom_iota = lax.broadcasted_iota(jnp.int32, (width, probes), 0)

    readt[...] = jnp.concatenate(
        [read_ref[...], jnp.zeros((8 - degrees, channels), f32)], axis=0
    ).T
    n_basis, units = w1t_ref.shape
    w1[...] = jnp.concatenate(
        [w1t_ref[...], jnp.zeros((n_basis, channels - units), f32)], axis=1
    ).T[:units]
    w2[...] = w2t_ref[...].astype(f32).T.astype(bf16)

    for i in range(chunks):
        for s in range(per):
            row = rows_s[i * per + s : i * per + s + 1, :]
            at = i * chunk + s * probes
            onehot[:, at : at + probes] = (atom_iota == row).astype(f32).astype(bf16)
        here = slice(i * chunk, (i + 1) * chunk)
        got = jnp.dot(win[...], onehot[:, here], preferred_element_type=f32)
        for s in range(per):
            j = i * per + s
            part = got[:, s * probes : (s + 1) * probes]
            at = i * chunk + s * probes
            feat[:, at : at + probes] = part[:channels] * wgt[j : j + 1, :]
            for k in range(3):
                xyz[k, j : j + 1, :] = part[channels + k : channels + k + 1]

    probe = probe_ref[...].astype(f32)
    dx = xyz[0] - probe[0:1]
    dy = xyz[1] - probe[1:2]
    dz = xyz[2] + slab_width * offset - probe[2:3]
    radius = jnp.sqrt(dx * dx + dy * dy + dz * dz + soften)
    rad_s[...] = radius
    for k, row in enumerate(harmonics(dx / radius, dy / radius, dz / radius)):
        sph[k] = row
    rows_k = degrees * degrees
    sph[rows_k] = wgt[...]
    centres = 0.75 * lax.broadcasted_iota(jnp.int32, (n_basis, probes), 0).astype(f32)

    for j in range(slots):
        shift = rad_s[j : j + 1, :] - centres
        basis[:, j * probes : (j + 1) * probes] = jnp.exp(-2.0 * (shift * shift))

    for i in range(chunks):
        at = slice(i * chunk, (i + 1) * chunk)
        for j in range(i * per, (i + 1) * per):
            for k in range(rows_k + 1):
                sphb[j, k] = jnp.broadcast_to(sph[k, j : j + 1, :], (8, probes))
        value = jnp.dot(w1[...], basis[:, at], precision=HIGH, preferred_element_type=f32)
        pre[:, at] = value
        hidden = (value * jax.nn.sigmoid(value)).astype(bf16)
        hid[:, at] = hidden
        radial[:, at] = jnp.dot(w2[...], hidden, preferred_element_type=f32)

    cot = jnp.broadcast_to(cot_ref[...], (8, probes))

    def channel_tile(t, dens):
        c0 = pl.multiple_of(t * 8, 8)

        def forward(j, acc):
            at = slice(j * probes, (j + 1) * probes)
            scaled = feat[pl.ds(c0, 8), at]
            acc = list(acc)
            for l in range(degrees):
                message = radial[pl.ds(l * channels + c0, 8), at] * scaled
                for k in range(l * l, (l + 1) * (l + 1)):
                    acc[k] = acc[k] + (message if k == 0 else sphb[j, k] * message)
            return acc

        zero = jnp.zeros((8, probes), f32)
        moment = [zero] * rows_k
        for j in range(slots):
            moment = forward(j, moment)
        grad = []
        for l in range(degrees):
            column = jnp.broadcast_to(readt[pl.ds(c0, 8), l : l + 1], (8, probes))
            if l == 0:
                squared = moment[0]
                grad.append(cot * column)
            else:
                squared = moment[l * l] * moment[l * l]
                for k in range(l * l + 1, (l + 1) * (l + 1)):
                    squared = squared + moment[k] * moment[k]
                factor = 2.0 * cot * column
                for k in range(l * l, (l + 1) * (l + 1)):
                    grad.append(factor * moment[k])
            squares[l, pl.ds(c0, 8), :] = squared
            dens = dens + column * squared

        for j in range(slots):
            at = slice(j * probes, (j + 1) * probes)
            scaled = feat[pl.ds(c0, 8), at]
            total_feat = None
            for l in range(degrees):
                message = None
                for k in range(l * l, (l + 1) * (l + 1)):
                    term = grad[k] if k == 0 else sphb[j, k] * grad[k]
                    message = term if message is None else message + term
                here = pl.ds(l * channels + c0, 8)
                term = message * radial[here, at]
                total_feat = term if total_feat is None else total_feat + term
                gradial[here, at] = message * scaled
            gfeat[pl.ds(c0, 8), at] = total_feat * sphb[j, rows_k]
        return dens

    dens = lax.fori_loop(0, channels // 8, channel_tile, jnp.zeros((8, probes), f32))
    dens_ref[...] = jnp.sum(dens, axis=0, keepdims=True)

    gwin_acc[...] = jnp.zeros_like(gwin_acc)
    gw2_acc[...] = jnp.zeros_like(gw2_acc)
    gw1_acc[...] = jnp.zeros_like(gw1_acc)

    for i in range(chunks):
        at = slice(i * chunk, (i + 1) * chunk)
        grads = gradial[:, at].astype(bf16)
        gw2_acc[...] += lax.dot_general(hid[:, at], grads, NT, preferred_element_type=f32)
        ghid = jnp.dot(w2t_ref[...], grads, preferred_element_type=f32)
        value = pre[:, at]
        logistic = jax.nn.sigmoid(value)
        gpre = ghid * logistic * (1.0 + value * (1.0 - logistic))
        gw1_acc[...] += lax.dot_general(
            basis[:, at], gpre, NT, precision=HIGH, preferred_element_type=f32
        )
        gwin_acc[...] += lax.dot_general(
            gfeat[:, at].astype(bf16), onehot[:, at], NT, preferred_element_type=f32
        )

    for b in range(blocks):
        gwin_ref[b] = gwin_acc[:, b * atoms : (b + 1) * atoms].astype(bf16)
    for l in range(degrees):
        pack_ref[l * units : (l + 1) * units] = gw2_acc[
            :, l * channels : (l + 1) * channels
        ].astype(bf16)
    half = degrees * units
    small = []
    for l in range(degrees):
        small.append(
            lax.dot_general(cot, squares[l], NT, precision=HIGH, preferred_element_type=f32)[:1]
        )
    small.append(jnp.zeros((8 - degrees, channels), f32))
    first = jnp.concatenate(small, axis=0)
    second = jnp.concatenate(
        [gw1_acc[...], jnp.zeros((n_basis, channels - units), f32)], axis=1
    )
    pack_ref[half : half + 16] = jnp.concatenate([first, second], axis=0).astype(bf16)
    rest = pack_ref.shape[0] - half - 16
    pack_ref[half + 16 :] = jnp.zeros((rest, channels), bf16)


def reduce_kernel(
    n_slab,
    n_plane,
    low,
    gwin_ref,
    pack_ref,
    gfeat_ref,
    out_ref,
    mine,
    land,
    part_b,
    part_c,
    land_a,
    land_b,
    land_c,
    halo_send,
    halo_recv,
    a_send,
    a_recv,
    b_send,
    b_recv,
    c_send,
    c_recv,
    own_sem,
):
    slab, plane, peers = halo_peers(n_slab, n_plane)
    group, high = low * n_plane, n_slab // low
    size = pack_ref.shape[0] // group
    slab_low, slab_high = lax.rem(slab, low), slab // low
    me = slab_low * n_plane + plane
    near = []
    for t in range(1, group):
        to = lax.rem(me + t, group)
        near.append((to, (slab - slab_low + to // n_plane, lax.rem(to, n_plane))))
    far = []
    for t in range(1, high):
        to = lax.rem(slab_high + t, high)
        far.append((to * low + slab_low, plane))
    own_rows = pl.ds(pl.multiple_of(me * size, 16), size)
    own_pack = pltpu.make_async_copy(pack_ref.at[own_rows], mine, own_sem.at[0])
    own_pack.start()
    own_block = n_plane + plane
    own_gwin = pltpu.make_async_copy(gwin_ref.at[own_block], land.at[own_block], own_sem.at[1])
    own_gwin.start()
    barrier = pltpu.get_barrier_semaphore()
    everyone = [(p[2], p[3]) for p in peers] + [n[1] for n in near] + far
    for device in everyone:
        pl.semaphore_signal(barrier, inc=1, device_id=device, device_id_type=MESH)
    pl.semaphore_wait(barrier, len(everyone))

    def send(source, target, send_sem, recv_sem, device):
        copy = pltpu.make_async_remote_copy(
            src_ref=source,
            dst_ref=target,
            send_sem=send_sem,
            recv_sem=recv_sem,
            device_id=device,
            device_id_type=MESH,
        )
        copy.start()
        return copy

    first = []
    for t, (to, device) in enumerate(near):
        rows = pl.ds(pl.multiple_of(to * size, 16), size)
        first.append(send(pack_ref.at[rows], land_a.at[t], a_send.at[t], a_recv.at[t], device))
    halo = []
    for t, (d, _, to_slab, to_plane) in enumerate(peers):
        halo.append(
            send(
                gwin_ref.at[(d + 1) * n_plane + to_plane],
                land.at[(d + 1) * n_plane + plane],
                halo_send.at[t],
                halo_recv.at[t],
                (to_slab, to_plane),
            )
        )
    own_pack.wait()
    own_gwin.wait()
    total = mine[...].astype(f32)
    for t, copy in enumerate(first):
        copy.wait_recv()
        total = total + land_a[t].astype(f32)
    part_b[...] = total
    land_b[slab_high] = total
    second = []
    for t, device in enumerate(far):
        second.append(
            send(part_b, land_b.at[slab_high], b_send.at[t], b_recv.at[t], device)
        )
    for copy in second:
        copy.wait_recv()
    total = land_b[0]
    for t in range(1, high):
        total = total + land_b[t]
    part_c[...] = total.astype(bf16)
    land_c[me] = total.astype(bf16)
    third = []
    for t, (_, device) in enumerate(near):
        third.append(send(part_c, land_c.at[me], c_send.at[t], c_recv.at[t], device))
    for copy in halo:
        copy.wait_recv()
    gfeat = land[0].astype(f32)
    for b in range(1, land.shape[0]):
        gfeat = gfeat + land[b].astype(f32)
    gfeat_ref[...] = gfeat
    for copy in third:
        copy.wait_recv()
    for b in range(group):
        out_ref[b * size : (b + 1) * size] = land_c[b]
    for copy in first + halo + second + third:
        copy.wait_send()


def finish_kernel(
    scale, feat_ref, pack_ref, gfeat_ref, gw1_ref, gw2_ref, gread_ref, full, sems
):
    copies = [
        pltpu.make_async_copy(pack_ref, full, sems.at[0]),
        pltpu.make_async_copy(feat_ref, gfeat_ref, sems.at[1]),
    ]
    for copy in copies:
        copy.start()
    copies[0].wait()
    units, channels = gw2_ref.shape[0], full.shape[1]
    degrees = gw2_ref.shape[1] // channels
    for l in range(degrees):
        rows = full[l * units : (l + 1) * units].astype(f32)
        gw2_ref[:, l * channels : (l + 1) * channels] = rows * scale
    half = degrees * units
    rows = full[half : half + 16].astype(f32) * scale
    gread_ref[...] = rows[: gread_ref.shape[0]]
    gw1_ref[...] = rows[8 : 8 + gw1_ref.shape[0], :units]
    copies[1].wait()


def shards(
    n_slab,
    n_plane,
    probe_pos,
    atom_pos,
    atom_feat,
    neighbours,
    valid,
    w_radial1,
    w_radial2,
    readout,
    cotangent,
):
    channels, atoms = atom_feat.shape
    slots, probes = neighbours.shape
    units, n_basis = w_radial1.shape
    degrees = readout.shape[0]
    out_rows = w_radial2.shape[0]
    half = degrees * units
    edges = slots * probes
    blocks = 3 * n_plane
    lines = -(-(channels + atom_pos.shape[0]) // 16) * 16
    peers = blocks - 1
    window = pl.pallas_call(
        functools.partial(halo_kernel, n_slab, n_plane),
        out_shape=jax.ShapeDtypeStruct((blocks, lines, atoms), bf16),
        in_specs=[VMEM] * 2,
        out_specs=VMEM,
        scratch_shapes=[
            pltpu.VMEM((lines, atoms), bf16),
            pltpu.VMEM((blocks, lines, atoms), bf16),
            pltpu.SemaphoreType.DMA((peers,)),
            pltpu.SemaphoreType.DMA((peers,)),
        ],
        compiler_params=pltpu.CompilerParams(collective_id=0, has_side_effects=True),
        name="halo",
    )(atom_feat, atom_pos)
    low = 4 if n_slab % 4 == 0 else 1
    group, high = low * n_plane, n_slab // low
    size = -(-(half + 16) // (16 * group)) * 16
    width = blocks * atoms
    kinds = degrees * degrees + 1
    density, gwin, pack = pl.pallas_call(
        functools.partial(edge_kernel, n_slab, n_plane),
        out_shape=(
            jax.ShapeDtypeStruct((1, probes), f32),
            jax.ShapeDtypeStruct((blocks, channels, atoms), bf16),
            jax.ShapeDtypeStruct((size * group, channels), bf16),
        ),
        in_specs=[VMEM] * 8,
        out_specs=(VMEM,) * 3,
        scratch_shapes=[
            pltpu.VMEM((lines, width), bf16),
            pltpu.VMEM((slots, probes), jnp.int32),
            pltpu.VMEM((slots, probes), f32),
            pltpu.VMEM((3, slots, probes), f32),
            pltpu.VMEM((width, edges), bf16),
            pltpu.VMEM((channels, edges), f32),
            pltpu.VMEM((channels, edges), f32),
            pltpu.VMEM((kinds, slots, probes), f32),
            pltpu.VMEM((slots, kinds, 8, probes), f32),
            pltpu.VMEM((slots, probes), f32),
            pltpu.VMEM((n_basis, edges), f32),
            pltpu.VMEM((units, edges), f32),
            pltpu.VMEM((units, edges), bf16),
            pltpu.VMEM((out_rows, edges), f32),
            pltpu.VMEM((out_rows, edges), f32),
            pltpu.VMEM((degrees, channels, probes), f32),
            pltpu.VMEM((channels, width), f32),
            pltpu.VMEM((units, out_rows), f32),
            pltpu.VMEM((n_basis, units), f32),
            pltpu.VMEM((channels, 8), f32),
            pltpu.VMEM((units, n_basis), f32),
            pltpu.VMEM((out_rows, units), bf16),
        ],
        compiler_params=pltpu.CompilerParams(vmem_limit_bytes=44 * 1024 * 1024),
        name="edges",
    )(
        window,
        neighbours,
        valid,
        probe_pos,
        cotangent.reshape(1, probes),
        w_radial1.T,
        w_radial2.T,
        readout,
    )
    feat_sum, pack_sum = pl.pallas_call(
        functools.partial(reduce_kernel, n_slab, n_plane, low),
        out_shape=(
            jax.ShapeDtypeStruct((channels, atoms), f32),
            jax.ShapeDtypeStruct((size * group, channels), bf16),
        ),
        in_specs=[ANY] * 2,
        out_specs=(VMEM,) * 2,
        scratch_shapes=[
            pltpu.VMEM((size, channels), bf16),
            pltpu.VMEM((blocks, channels, atoms), bf16),
            pltpu.VMEM((size, channels), f32),
            pltpu.VMEM((size, channels), bf16),
            pltpu.VMEM((group - 1, size, channels), bf16),
            pltpu.VMEM((high, size, channels), f32),
            pltpu.VMEM((group, size, channels), bf16),
            pltpu.SemaphoreType.DMA((peers,)),
            pltpu.SemaphoreType.DMA((peers,)),
            pltpu.SemaphoreType.DMA((group - 1,)),
            pltpu.SemaphoreType.DMA((group - 1,)),
            pltpu.SemaphoreType.DMA((high,)),
            pltpu.SemaphoreType.DMA((high,)),
            pltpu.SemaphoreType.DMA((group - 1,)),
            pltpu.SemaphoreType.DMA((group - 1,)),
            pltpu.SemaphoreType.DMA((2,)),
        ],
        compiler_params=pltpu.CompilerParams(collective_id=1, has_side_effects=True),
        name="reduce",
    )(gwin, pack)
    scale = 1.0 / math.sqrt(probes * n_slab * n_plane)
    grad_feat, grad_w1, grad_w2, grad_read = pl.pallas_call(
        functools.partial(finish_kernel, scale),
        out_shape=(
            jax.ShapeDtypeStruct((channels, atoms), f32),
            jax.ShapeDtypeStruct((n_basis, units), f32),
            jax.ShapeDtypeStruct((units, out_rows), f32),
            jax.ShapeDtypeStruct((degrees, channels), f32),
        ),
        in_specs=[ANY] * 2,
        out_specs=(VMEM,) * 4,
        scratch_shapes=[
            pltpu.VMEM((size * group, channels), bf16),
            pltpu.SemaphoreType.DMA((2,)),
        ],
        name="finish",
    )(feat_sum, pack_sum)
    return density.reshape(-1), grad_feat, grad_w1.T, grad_w2.T, grad_read


def solution(mesh):
    both = P(None, ("slab", "plane"))
    in_specs = (both,) * 5 + (P(), P(), P(), P(("slab", "plane")))
    out_specs = (P(("slab", "plane")), both, P(), P(), P())
    body = functools.partial(shards, mesh.shape["slab"], mesh.shape["plane"])
    return jax.shard_map(
        body, mesh=mesh, in_specs=in_specs, out_specs=out_specs, check_vma=False
    )
```

```python
import functools
import math

import jax
import jax.numpy as jnp
from jax import lax
from jax.experimental import pallas as pl
from jax.experimental.pallas import tpu as pltpu
from jax.sharding import PartitionSpec as P

slab_width = 2.0
soften = 0.25
f32 = jnp.float32
bf16 = jnp.bfloat16
MESH = pl.DeviceIdType.MESH
HIGH = lax.Precision.HIGHEST
VMEM = pl.BlockSpec(memory_space=pltpu.VMEM)
HBM = pl.BlockSpec(memory_space=pltpu.HBM)
ANY = pl.BlockSpec(memory_space=pl.ANY)
NT = (((1,), (1,)), ((), ()))


def harmonics(x, y, z):
    xx, yy, zz = x * x, y * y, z * z
    r3, r5, r15 = math.sqrt(3.0), math.sqrt(5.0), math.sqrt(15.0)
    a1, a2 = math.sqrt(35.0 / 8.0), math.sqrt(105.0)
    a3, a4 = math.sqrt(21.0 / 8.0), math.sqrt(7.0) / 2.0
    b1, b2 = 3.0 * math.sqrt(35.0) / 2.0, 3.0 * math.sqrt(70.0) / 4.0
    b3, b4 = 3.0 * math.sqrt(5.0) / 2.0, 3.0 * math.sqrt(10.0) / 4.0
    return [
        jnp.ones_like(x),
        r3 * y,
        r3 * z,
        r3 * x,
        r15 * x * y,
        r15 * y * z,
        r5 / 2.0 * (3.0 * zz - 1.0),
        r15 * x * z,
        r15 / 2.0 * (xx - yy),
        a1 * y * (3.0 * xx - yy),
        a2 * x * y * z,
        a3 * y * (5.0 * zz - 1.0),
        a4 * z * (5.0 * zz - 3.0),
        a3 * x * (5.0 * zz - 1.0),
        a2 / 2.0 * z * (xx - yy),
        a1 * x * (xx - 3.0 * yy),
        b1 * x * y * (xx - yy),
        b2 * y * z * (3.0 * xx - yy),
        b3 * x * y * (7.0 * zz - 1.0),
        b4 * y * z * (7.0 * zz - 3.0),
        0.375 * (35.0 * zz * zz - 30.0 * zz + 3.0),
        b4 * x * z * (7.0 * zz - 3.0),
        b3 / 2.0 * (xx - yy) * (7.0 * zz - 1.0),
        b2 * x * z * (xx - 3.0 * yy),
        b1 / 4.0 * (xx * (xx - 3.0 * yy) - yy * (3.0 * xx - yy)),
    ]


def halo_peers(n_slab, n_plane):
    slab, plane = lax.axis_index("slab"), lax.axis_index("plane")
    peers = []
    for d in (-1, 0, 1):
        for q in range(n_plane):
            if d == 0 and q == 0:
                continue
            to_slab = lax.rem(slab + d + n_slab, n_slab)
            to_plane = lax.rem(plane + q, n_plane)
            peers.append((d, q, to_slab, to_plane))
    return slab, plane, peers


def halo_kernel(n_slab, n_plane, feat_ref, pos_ref, out_ref, own, land, send_sem, recv_sem):
    slab, plane, peers = halo_peers(n_slab, n_plane)
    barrier = pltpu.get_barrier_semaphore()
    for _, _, to_slab, to_plane in peers:
        pl.semaphore_signal(barrier, inc=1, device_id=(to_slab, to_plane), device_id_type=MESH)
    channels = feat_ref.shape[0]
    rest = own.shape[0] - channels - pos_ref.shape[0]
    own[0:channels] = feat_ref[...]
    own[channels:] = jnp.concatenate(
        [pos_ref[...].astype(f32), jnp.zeros((rest, own.shape[1]), f32)], axis=0
    ).astype(bf16)
    pl.semaphore_wait(barrier, len(peers))
    copies = []
    for number, (d, _, to_slab, to_plane) in enumerate(peers):
        copy = pltpu.make_async_remote_copy(
            src_ref=own,
            dst_ref=land.at[(1 - d) * n_plane + plane],
            send_sem=send_sem.at[number],
            recv_sem=recv_sem.at[number],
            device_id=(to_slab, to_plane),
            device_id_type=MESH,
        )
        copy.start()
        copies.append(copy)
    land[n_plane + plane] = own[...]
    for copy in copies:
        copy.wait()
    out_ref[...] = land[...]


def edge_kernel(
    n_slab,
    n_plane,
    win_ref,
    nbr_ref,
    valid_ref,
    probe_ref,
    cot_ref,
    w1t_ref,
    w2t_ref,
    read_ref,
    dens_ref,
    gwin_ref,
    pack_ref,
    win,
    rows_s,
    wgt,
    xyz,
    onehot,
    feat,
    gfeat,
    sph,
    sphb,
    rad_s,
    basis,
    pre,
    hid,
    radial,
    gradial,
    squares,
    gwin_acc,
    gw2_acc,
    gw1_acc,
    readt,
    w1,
    w2,
):
    slots, probes = nbr_ref.shape
    blocks, _, atoms = win_ref.shape
    width = blocks * atoms
    atom_slab = n_plane * atoms
    channels = feat.shape[0]
    degrees = read_ref.shape[0]
    per = 4
    chunk = per * probes
    chunks = slots // per
    total = n_slab * atom_slab
    for b in range(blocks):
        win[:, b * atoms : (b + 1) * atoms] = win_ref[b]
    local = nbr_ref[...] - (lax.axis_index("slab") - 1) * atom_slab
    local = jnp.where(local < 0, local + total, local)
    local = jnp.where(local >= total, local - total, local)
    rows_s[...] = local
    wgt[...] = valid_ref[...].astype(f32) * (1.0 / math.sqrt(slots))
    offset = jnp.where(local < atom_slab, -1.0, jnp.where(local < 2 * atom_slab, 0.0, 1.0))
    atom_iota = lax.broadcasted_iota(jnp.int32, (width, probes), 0)

    readt[...] = jnp.concatenate(
        [read_ref[...], jnp.zeros((8 - degrees, channels), f32)], axis=0
    ).T
    n_basis, units = w1t_ref.shape
    w1[...] = jnp.concatenate(
        [w1t_ref[...], jnp.zeros((n_basis, channels - units), f32)], axis=1
    ).T[:units]
    w2[...] = w2t_ref[...].astype(f32).T.astype(bf16)

    for i in range(chunks):
        for s in range(per):
            row = rows_s[i * per + s : i * per + s + 1, :]
            at = i * chunk + s * probes
            onehot[:, at : at + probes] = (atom_iota == row).astype(f32).astype(bf16)
        here = slice(i * chunk, (i + 1) * chunk)
        got = jnp.dot(win[...], onehot[:, here], preferred_element_type=f32)
        for s in range(per):
            j = i * per + s
            part = got[:, s * probes : (s + 1) * probes]
            at = i * chunk + s * probes
            feat[:, at : at + probes] = part[:channels] * wgt[j : j + 1, :]
            for k in range(3):
                xyz[k, j : j + 1, :] = part[channels + k : channels + k + 1]

    probe = probe_ref[...].astype(f32)
    dx = xyz[0] - probe[0:1]
    dy = xyz[1] - probe[1:2]
    dz = xyz[2] + slab_width * offset - probe[2:3]
    radius = jnp.sqrt(dx * dx + dy * dy + dz * dz + soften)
    rad_s[...] = radius
    for k, row in enumerate(harmonics(dx / radius, dy / radius, dz / radius)):
        sph[k] = row
    rows_k = degrees * degrees
    sph[rows_k] = wgt[...]
    centres = 0.75 * lax.broadcasted_iota(jnp.int32, (n_basis, probes), 0).astype(f32)

    for j in range(slots):
        shift = rad_s[j : j + 1, :] - centres
        basis[:, j * probes : (j + 1) * probes] = jnp.exp(-2.0 * (shift * shift))

    for i in range(chunks):
        at = slice(i * chunk, (i + 1) * chunk)
        for j in range(i * per, (i + 1) * per):
            for k in range(rows_k + 1):
                sphb[j, k] = jnp.broadcast_to(sph[k, j : j + 1, :], (8, probes))
        value = jnp.dot(w1[...], basis[:, at], precision=HIGH, preferred_element_type=f32)
        pre[:, at] = value
        hidden = (value * jax.nn.sigmoid(value)).astype(bf16)
        hid[:, at] = hidden
        radial[:, at] = jnp.dot(w2[...], hidden, preferred_element_type=f32)

    cot = jnp.broadcast_to(cot_ref[...], (8, probes))

    pair = range(2)
    groups = (tuple(range(degrees - 1)), (degrees - 1,))

    def orders(l):
        return range(l * l, (l + 1) * (l + 1))

    def channel_pair(t, dens):
        starts = [pl.multiple_of(t * 16 + 8 * h, 8) for h in pair]
        zero = jnp.zeros((8, probes), f32)
        moment = [[zero] * rows_k for _ in pair]
        for group in groups:
            for j in range(slots):
                at = slice(j * probes, (j + 1) * probes)
                scaled = [feat[pl.ds(c, 8), at] for c in starts]
                for l in group:
                    message = [
                        radial[pl.ds(l * channels + starts[h], 8), at] * scaled[h] for h in pair
                    ]
                    for k in orders(l):
                        factor = None if k == 0 else sphb[j, k]
                        for h in pair:
                            term = message[h] if k == 0 else factor * message[h]
                            moment[h][k] = moment[h][k] + term
        grad = [[None] * rows_k for _ in pair]
        for h in pair:
            for l in range(degrees):
                rows = pl.ds(starts[h], 8)
                column = jnp.broadcast_to(readt[rows, l : l + 1], (8, probes))
                if l == 0:
                    squared = moment[h][0]
                    grad[h][0] = cot * column
                else:
                    squared = None
                    factor = 2.0 * cot * column
                    for k in orders(l):
                        term = moment[h][k] * moment[h][k]
                        squared = term if squared is None else squared + term
                        grad[h][k] = factor * moment[h][k]
                squares[l, rows, :] = squared
                dens = dens + column * squared
        for number, group in enumerate(groups):
            for j in range(slots):
                at = slice(j * probes, (j + 1) * probes)
                scaled = [feat[pl.ds(c, 8), at] for c in starts]
                total = [None for _ in pair]
                for l in group:
                    message = [None for _ in pair]
                    for k in orders(l):
                        factor = None if k == 0 else sphb[j, k]
                        for h in pair:
                            term = grad[h][k] if k == 0 else factor * grad[h][k]
                            message[h] = term if message[h] is None else message[h] + term
                    for h in pair:
                        here = pl.ds(l * channels + starts[h], 8)
                        term = message[h] * radial[here, at]
                        total[h] = term if total[h] is None else total[h] + term
                        gradial[here, at] = message[h] * scaled[h]
                for h in pair:
                    rows = pl.ds(starts[h], 8)
                    if number == 0:
                        gfeat[rows, at] = total[h]
                    else:
                        gfeat[rows, at] = (gfeat[rows, at] + total[h]) * sphb[j, rows_k]
        return dens

    dens = lax.fori_loop(0, channels // 16, channel_pair, jnp.zeros((8, probes), f32))
    dens_ref[...] = jnp.sum(dens, axis=0, keepdims=True)

    gwin_acc[...] = jnp.zeros_like(gwin_acc)
    gw2_acc[...] = jnp.zeros_like(gw2_acc)
    gw1_acc[...] = jnp.zeros_like(gw1_acc)

    for i in range(chunks):
        at = slice(i * chunk, (i + 1) * chunk)
        grads = gradial[:, at].astype(bf16)
        gw2_acc[...] += lax.dot_general(hid[:, at], grads, NT, preferred_element_type=f32)
        ghid = jnp.dot(w2t_ref[...], grads, preferred_element_type=f32)
        value = pre[:, at]
        logistic = jax.nn.sigmoid(value)
        gpre = ghid * logistic * (1.0 + value * (1.0 - logistic))
        gw1_acc[...] += lax.dot_general(
            basis[:, at], gpre, NT, precision=HIGH, preferred_element_type=f32
        )
        gwin_acc[...] += lax.dot_general(
            gfeat[:, at].astype(bf16), onehot[:, at], NT, preferred_element_type=f32
        )

    for b in range(blocks):
        gwin_ref[b] = gwin_acc[:, b * atoms : (b + 1) * atoms].astype(bf16)
    for l in range(degrees):
        pack_ref[l * units : (l + 1) * units] = gw2_acc[
            :, l * channels : (l + 1) * channels
        ].astype(bf16)
    half = degrees * units
    small = []
    for l in range(degrees):
        small.append(
            lax.dot_general(cot, squares[l], NT, precision=HIGH, preferred_element_type=f32)[:1]
        )
    small.append(jnp.zeros((8 - degrees, channels), f32))
    first = jnp.concatenate(small, axis=0)
    second = jnp.concatenate(
        [gw1_acc[...], jnp.zeros((n_basis, channels - units), f32)], axis=1
    )
    pack_ref[half : half + 16] = jnp.concatenate([first, second], axis=0).astype(bf16)
    rest = pack_ref.shape[0] - half - 16
    pack_ref[half + 16 :] = jnp.zeros((rest, channels), bf16)


def reduce_kernel(
    n_slab,
    n_plane,
    low,
    gwin_ref,
    pack_ref,
    gfeat_ref,
    out_ref,
    mine,
    land,
    part_b,
    part_c,
    land_a,
    land_b,
    land_c,
    halo_send,
    halo_recv,
    a_send,
    a_recv,
    b_send,
    b_recv,
    c_send,
    c_recv,
    own_sem,
):
    slab, plane, peers = halo_peers(n_slab, n_plane)
    group, high = low * n_plane, n_slab // low
    size = pack_ref.shape[0] // group
    slab_low, slab_high = lax.rem(slab, low), slab // low
    me = slab_low * n_plane + plane
    near = []
    for t in range(1, group):
        to = lax.rem(me + t, group)
        near.append((to, (slab - slab_low + to // n_plane, lax.rem(to, n_plane))))
    far = []
    for t in range(1, high):
        to = lax.rem(slab_high + t, high)
        far.append((to * low + slab_low, plane))
    own_rows = pl.ds(pl.multiple_of(me * size, 16), size)
    own_pack = pltpu.make_async_copy(pack_ref.at[own_rows], mine, own_sem.at[0])
    own_pack.start()
    own_block = n_plane + plane
    own_gwin = pltpu.make_async_copy(gwin_ref.at[own_block], land.at[own_block], own_sem.at[1])
    own_gwin.start()
    barrier = pltpu.get_barrier_semaphore()
    everyone = [(p[2], p[3]) for p in peers] + [n[1] for n in near] + far
    for device in everyone:
        pl.semaphore_signal(barrier, inc=1, device_id=device, device_id_type=MESH)
    pl.semaphore_wait(barrier, len(everyone))

    def send(source, target, send_sem, recv_sem, device):
        copy = pltpu.make_async_remote_copy(
            src_ref=source,
            dst_ref=target,
            send_sem=send_sem,
            recv_sem=recv_sem,
            device_id=device,
            device_id_type=MESH,
        )
        copy.start()
        return copy

    first = []
    for t, (to, device) in enumerate(near):
        rows = pl.ds(pl.multiple_of(to * size, 16), size)
        first.append(send(pack_ref.at[rows], land_a.at[t], a_send.at[t], a_recv.at[t], device))
    halo = []
    for t, (d, _, to_slab, to_plane) in enumerate(peers):
        halo.append(
            send(
                gwin_ref.at[(d + 1) * n_plane + to_plane],
                land.at[(d + 1) * n_plane + plane],
                halo_send.at[t],
                halo_recv.at[t],
                (to_slab, to_plane),
            )
        )
    own_pack.wait()
    own_gwin.wait()
    total = mine[...].astype(f32)
    for t, copy in enumerate(first):
        copy.wait_recv()
        total = total + land_a[t].astype(f32)
    part_b[...] = total
    land_b[slab_high] = total
    second = []
    for t, device in enumerate(far):
        second.append(
            send(part_b, land_b.at[slab_high], b_send.at[t], b_recv.at[t], device)
        )
    for copy in second:
        copy.wait_recv()
    total = land_b[0]
    for t in range(1, high):
        total = total + land_b[t]
    part_c[...] = total.astype(bf16)
    land_c[me] = total.astype(bf16)
    third = []
    for t, (_, device) in enumerate(near):
        third.append(send(part_c, land_c.at[me], c_send.at[t], c_recv.at[t], device))
    for copy in halo:
        copy.wait_recv()
    gfeat = land[0].astype(f32)
    for b in range(1, land.shape[0]):
        gfeat = gfeat + land[b].astype(f32)
    gfeat_ref[...] = gfeat
    for copy in third:
        copy.wait_recv()
    for b in range(group):
        out_ref[b * size : (b + 1) * size] = land_c[b]
    for copy in first + halo + second + third:
        copy.wait_send()


def finish_kernel(
    scale, feat_ref, pack_ref, gfeat_ref, gw1_ref, gw2_ref, gread_ref, full, sems
):
    copies = [
        pltpu.make_async_copy(pack_ref, full, sems.at[0]),
        pltpu.make_async_copy(feat_ref, gfeat_ref, sems.at[1]),
    ]
    for copy in copies:
        copy.start()
    copies[0].wait()
    units, channels = gw2_ref.shape[0], full.shape[1]
    degrees = gw2_ref.shape[1] // channels
    for l in range(degrees):
        rows = full[l * units : (l + 1) * units].astype(f32)
        gw2_ref[:, l * channels : (l + 1) * channels] = rows * scale
    half = degrees * units
    rows = full[half : half + 16].astype(f32) * scale
    gread_ref[...] = rows[: gread_ref.shape[0]]
    gw1_ref[...] = rows[8 : 8 + gw1_ref.shape[0], :units]
    copies[1].wait()


def shards(
    n_slab,
    n_plane,
    probe_pos,
    atom_pos,
    atom_feat,
    neighbours,
    valid,
    w_radial1,
    w_radial2,
    readout,
    cotangent,
):
    channels, atoms = atom_feat.shape
    slots, probes = neighbours.shape
    units, n_basis = w_radial1.shape
    degrees = readout.shape[0]
    out_rows = w_radial2.shape[0]
    half = degrees * units
    edges = slots * probes
    blocks = 3 * n_plane
    lines = -(-(channels + atom_pos.shape[0]) // 16) * 16
    peers = blocks - 1
    window = pl.pallas_call(
        functools.partial(halo_kernel, n_slab, n_plane),
        out_shape=jax.ShapeDtypeStruct((blocks, lines, atoms), bf16),
        in_specs=[VMEM] * 2,
        out_specs=VMEM,
        scratch_shapes=[
            pltpu.VMEM((lines, atoms), bf16),
            pltpu.VMEM((blocks, lines, atoms), bf16),
            pltpu.SemaphoreType.DMA((peers,)),
            pltpu.SemaphoreType.DMA((peers,)),
        ],
        compiler_params=pltpu.CompilerParams(collective_id=0, has_side_effects=True),
        name="halo",
    )(atom_feat, atom_pos)
    low = 4 if n_slab % 4 == 0 else 1
    group, high = low * n_plane, n_slab // low
    size = -(-(half + 16) // (16 * group)) * 16
    width = blocks * atoms
    kinds = degrees * degrees + 1
    density, gwin, pack = pl.pallas_call(
        functools.partial(edge_kernel, n_slab, n_plane),
        out_shape=(
            jax.ShapeDtypeStruct((1, probes), f32),
            jax.ShapeDtypeStruct((blocks, channels, atoms), bf16),
            jax.ShapeDtypeStruct((size * group, channels), bf16),
        ),
        in_specs=[VMEM] * 8,
        out_specs=(VMEM,) * 3,
        scratch_shapes=[
            pltpu.VMEM((lines, width), bf16),
            pltpu.VMEM((slots, probes), jnp.int32),
            pltpu.VMEM((slots, probes), f32),
            pltpu.VMEM((3, slots, probes), f32),
            pltpu.VMEM((width, edges), bf16),
            pltpu.VMEM((channels, edges), f32),
            pltpu.VMEM((channels, edges), f32),
            pltpu.VMEM((kinds, slots, probes), f32),
            pltpu.VMEM((slots, kinds, 8, probes), f32),
            pltpu.VMEM((slots, probes), f32),
            pltpu.VMEM((n_basis, edges), f32),
            pltpu.VMEM((units, edges), f32),
            pltpu.VMEM((units, edges), bf16),
            pltpu.VMEM((out_rows, edges), f32),
            pltpu.VMEM((out_rows, edges), f32),
            pltpu.VMEM((degrees, channels, probes), f32),
            pltpu.VMEM((channels, width), f32),
            pltpu.VMEM((units, out_rows), f32),
            pltpu.VMEM((n_basis, units), f32),
            pltpu.VMEM((channels, 8), f32),
            pltpu.VMEM((units, n_basis), f32),
            pltpu.VMEM((out_rows, units), bf16),
        ],
        compiler_params=pltpu.CompilerParams(vmem_limit_bytes=44 * 1024 * 1024),
        name="edges",
    )(
        window,
        neighbours,
        valid,
        probe_pos,
        cotangent.reshape(1, probes),
        w_radial1.T,
        w_radial2.T,
        readout,
    )
    feat_sum, pack_sum = pl.pallas_call(
        functools.partial(reduce_kernel, n_slab, n_plane, low),
        out_shape=(
            jax.ShapeDtypeStruct((channels, atoms), f32),
            jax.ShapeDtypeStruct((size * group, channels), bf16),
        ),
        in_specs=[HBM] * 2,
        out_specs=(VMEM,) * 2,
        scratch_shapes=[
            pltpu.VMEM((size, channels), bf16),
            pltpu.VMEM((blocks, channels, atoms), bf16),
            pltpu.VMEM((size, channels), f32),
            pltpu.VMEM((size, channels), bf16),
            pltpu.VMEM((group - 1, size, channels), bf16),
            pltpu.VMEM((high, size, channels), f32),
            pltpu.VMEM((group, size, channels), bf16),
            pltpu.SemaphoreType.DMA((peers,)),
            pltpu.SemaphoreType.DMA((peers,)),
            pltpu.SemaphoreType.DMA((group - 1,)),
            pltpu.SemaphoreType.DMA((group - 1,)),
            pltpu.SemaphoreType.DMA((high,)),
            pltpu.SemaphoreType.DMA((high,)),
            pltpu.SemaphoreType.DMA((group - 1,)),
            pltpu.SemaphoreType.DMA((group - 1,)),
            pltpu.SemaphoreType.DMA((2,)),
        ],
        compiler_params=pltpu.CompilerParams(collective_id=1, has_side_effects=True),
        name="reduce",
    )(gwin, pack)
    scale = 1.0 / math.sqrt(probes * n_slab * n_plane)
    grad_feat, grad_w1, grad_w2, grad_read = pl.pallas_call(
        functools.partial(finish_kernel, scale),
        out_shape=(
            jax.ShapeDtypeStruct((channels, atoms), f32),
            jax.ShapeDtypeStruct((n_basis, units), f32),
            jax.ShapeDtypeStruct((units, out_rows), f32),
            jax.ShapeDtypeStruct((degrees, channels), f32),
        ),
        in_specs=[ANY] * 2,
        out_specs=(VMEM,) * 4,
        scratch_shapes=[
            pltpu.VMEM((size * group, channels), bf16),
            pltpu.SemaphoreType.DMA((2,)),
        ],
        name="finish",
    )(feat_sum, pack_sum)
    return density.reshape(-1), grad_feat, grad_w1.T, grad_w2.T, grad_read


def solution(mesh):
    both = P(None, ("slab", "plane"))
    in_specs = (both,) * 5 + (P(), P(), P(), P(("slab", "plane")))
    out_specs = (P(("slab", "plane")), both, P(), P(), P())
    body = functools.partial(shards, mesh.shape["slab"], mesh.shape["plane"])
    return jax.shard_map(
        body, mesh=mesh, in_specs=in_specs, out_specs=out_specs, check_vma=False
    )
```
